256 devices in a mesh: comp: 128 (over x, y, z), blk: 2 (over core).
Axes of the slice: x: 4, y: 4, z: 8, core: 2. Of those that a mesh axis runs over, the one named last changes fastest.
Arguments:
- constraint_modes: bfloat16 [128, 2048, 1024], P('comp', 'blk'), may hold values from -6 to 6
- stiff_blocks: bfloat16 [128, 2048, 512], P('comp', 'blk'), may hold values from -0.25 to 0.25
- block_cols: int32 [128, 32, 8], P('comp', 'blk'), may hold values from 0 to 31, as said below
- flange_rows: int32 [128, 252], P('comp', 'blk'), may hold values from 0 to 1023, as said below
- flange_dest: int32 [128, 252], P('comp', 'blk'), may hold values from 0 to 127, as said below
- flange_match: int32 [128, 252], P('comp', 'blk'), may hold values from 0 to 251, as said below
- flange_stiff: float32 [128, 252], P('comp', 'blk'), may hold values from 0.3 to 3
- joint_rows: int32 [128, 512], P('comp', 'blk'), may hold values from 0 to 1023
- joint_owner: int32 [128, 512], P('comp', 'blk'), may hold values from 0 to 127, as said below
- joint_local: int32 [128, 512], P('comp', 'blk'), may hold values from 0 to 63
Outputs:
- reduced_stiff: float32 [128, 1024, 1024], P('comp', None, 'blk')
- joint_forces: float32 [8192, 1024], P('comp', 'blk')
The draws below stay inside these ranges and needn't reach their ends.
Inputs may be any that keep to these rules, and one draw needn't show every extreme that they name: `block_cols`: the 8 block columns of one block row are different. `flange_rows`: the flange rows of one half of a component are different rows of that half. `flange_dest`: within each half of a component the entries form 63 groups of 2 consecutive entries; all entries of a group pair with the entries of one group of one other component in the same half, and the groups of one half pair with different components. `flange_match`: the pairing is mutual: if entry n of c names entry m of p, then entry m of p names entry n of c. `joint_owner`: at most 4 of the 256 entries of one half of a component name one owner, and one owner is named exactly 4 times by every half of every component.
All inputs are finite; a program needn't handle non-finite values.
Results may differ from the reference program's by a relative error of at most 0.0028.
Values may be sent and summed in bfloat16 or wider, within the bound.
A program may use at most 128 MiB of HBM per device.

```python
import math
import jax
import jax.numpy as jnp
from jax import lax

IFACE = 1024
BLOCK = 64
NEIGH = 8
ROWS_DEV = 1024
FCAP = 2
JCAP = 4
JOWN = 64
COMPONENTS = 128
ROWS = 2048
BROWS = 32
FGROUPS = 63
FN_DEV = 126
FNODES = 252
JS_DEV = 256
JSLOTS = 512
JOINTS = 8192


def draw_block_cols(key, part):
    subkeys = jax.random.split(jax.random.fold_in(key, 5), COMPONENTS * BROWS)

    def one_row(subkey):
        return jax.random.permutation(subkey, BROWS)[:NEIGH]
    return jax.vmap(one_row)(subkeys).reshape(COMPONENTS, BROWS, NEIGH).astype(jnp.int32)


def draw_flange_rows(key, part):
    halves = FNODES // FN_DEV
    subkeys = jax.random.split(jax.random.fold_in(key, 31), COMPONENTS * halves)

    def one_half(subkey):
        return jax.random.permutation(subkey, ROWS_DEV)[:FN_DEV]
    return jax.vmap(one_half)(subkeys).reshape(COMPONENTS, FNODES).astype(jnp.int32)


def flange_tables(key):
    halves = FNODES // FN_DEV
    half_groups = (FGROUPS + 1) // 2
    drawn = jax.random.permutation(jax.random.fold_in(key, 11), jnp.arange(1, COMPONENTS // 2, dtype=jnp.int32))[:half_groups - 1]
    shifts = jnp.concatenate([drawn, jnp.full((1,), COMPONENTS // 2, jnp.int32)])
    shape_all = (COMPONENTS, halves, FGROUPS, FCAP)
    comp_ids = jnp.broadcast_to(jnp.arange(COMPONENTS, dtype=jnp.int32)[:, None, None, None], shape_all)
    half_ids = jnp.broadcast_to(jnp.arange(halves, dtype=jnp.int32)[None, :, None, None], shape_all)
    group_ids = jnp.broadcast_to(jnp.arange(FGROUPS, dtype=jnp.int32)[None, None, :, None], shape_all)
    node_ids = jnp.broadcast_to(jnp.arange(FCAP, dtype=jnp.int32)[None, None, None, :], shape_all)
    first = group_ids == 0
    lower = group_ids < half_groups
    base_group = jnp.where(first, half_groups - 1, jnp.where(lower, group_ids - 1, group_ids - half_groups))
    offset = shifts[base_group]
    partner = jnp.where(lower, (comp_ids + offset) % COMPONENTS, (comp_ids - offset) % COMPONENTS)
    partner_group = jnp.where(first, 0, jnp.where(lower, group_ids + half_groups - 1, group_ids - half_groups + 1))
    subkeys = jax.random.split(jax.random.fold_in(key, 12), COMPONENTS * halves * half_groups)

    def one_perm(subkey):
        return jax.random.permutation(subkey, FCAP).astype(jnp.int32)
    perms = jax.vmap(one_perm)(subkeys).reshape(COMPONENTS, halves, half_groups, FCAP)
    inverse = jnp.argsort(perms, axis=-1).astype(jnp.int32)
    forward_pick = perms[comp_ids, half_ids, base_group, node_ids]
    backward_pick = inverse[partner, half_ids, base_group, node_ids]
    use_forward = jnp.where(first, comp_ids < COMPONENTS // 2, lower)
    position = jnp.where(use_forward, forward_pick, backward_pick)
    match_entry = half_ids * FN_DEV + partner_group * FCAP + position
    return (partner.reshape(COMPONENTS, FNODES).astype(jnp.int32), match_entry.reshape(COMPONENTS, FNODES).astype(jnp.int32))


def draw_flange_dest(key, part):
    return flange_tables(key)[0]


def draw_flange_match(key, part):
    return flange_tables(key)[1]


def draw_joint_owner(key, part):
    halves = JSLOTS // JS_DEV
    hottest = jax.random.randint(jax.random.fold_in(key, 21), (), 0, COMPONENTS).astype(jnp.int32)
    tokens = jnp.arange((COMPONENTS - 1) * JCAP, dtype=jnp.int32) // JCAP
    tokens = tokens + (tokens >= hottest).astype(jnp.int32)
    subkeys = jax.random.split(jax.random.fold_in(key, 22), COMPONENTS * halves)

    def one_half(subkey):
        first_key, second_key = jax.random.split(subkey)
        others = jax.random.permutation(first_key, tokens)[:JS_DEV - JCAP]
        filled = jnp.concatenate([jnp.full((JCAP,), hottest, jnp.int32), others])
        return jax.random.permutation(second_key, filled)
    return jax.vmap(one_half)(subkeys).reshape(COMPONENTS, JSLOTS).astype(jnp.int32)


def touch_ends(entries, key, smallest, high):
    shape = entries.shape
    index_at = [jax.random.randint(jax.random.fold_in(key, axis), (), 0, shape[axis]) for axis in range(len(shape))]
    entries = entries.at[tuple(index_at)].set(smallest)
    longest = shape.index(max(shape))
    index_at[longest] = (index_at[longest] + 1) % shape[longest]
    return entries.at[tuple(index_at)].set(high)


def level_of(key, shape, cuts, least, largest):
    def one(axis_at, blocks):
        steps = jax.random.uniform(jax.random.fold_in(jax.random.fold_in(key, 6), axis_at), (blocks,), jnp.float32, least / len(cuts), largest / len(cuts))
        return jnp.repeat(jnp.exp(steps), shape[axis_at] // blocks).reshape((-1,) + (1,) * (len(shape) - axis_at - 1))

    loudness = one(*cuts[0])
    for cut in cuts[1:]:
        loudness = loudness * one(*cut)
    return loudness


def centred(stream_key, shape, spread, most, cuts=(), kind=jnp.bfloat16):
    values = jax.random.normal(stream_key, shape, jnp.float32) * spread
    if len(cuts) > 0:
        values = level_of(stream_key, shape, cuts, -0.22, 0.18) * values
    return jnp.clip(values, min=-most, max=most).astype(kind)


def setup_inputs(seed: int = 0) -> dict:
    keys = jax.random.split(jax.random.key(seed), 11)
    return {
        "constraint_modes": centred(keys[0], (COMPONENTS, ROWS, IFACE), 1.0, 6.0, ((0, 128), (1, 2))),
        "stiff_blocks": centred(keys[1], (COMPONENTS, ROWS, NEIGH * BLOCK), (NEIGH * BLOCK) ** -0.5, 0.25, ((0, 128), (1, 2))),
        "block_cols": draw_block_cols(jax.random.fold_in(keys[10], 71), 0),
        "flange_rows": draw_flange_rows(jax.random.fold_in(keys[10], 71), 0),
        "flange_dest": draw_flange_dest(jax.random.fold_in(keys[10], 71), 0),
        "flange_match": draw_flange_match(jax.random.fold_in(keys[10], 71), 0),
        "flange_stiff": jnp.clip(jnp.exp(math.log(3.0) - 2.3025851 * jax.random.uniform(keys[6], (COMPONENTS, FNODES), jnp.float32) ** level_of(keys[6], (COMPONENTS, FNODES), ((0, 128), (1, 2)), -0.2, 0.2)), 0.3, 3.0),
        "joint_rows": touch_ends(jax.random.randint(keys[7], (COMPONENTS, JSLOTS), 0, ROWS_DEV), jax.random.fold_in(keys[7], 1), 0, ROWS_DEV - 1).astype(jnp.int32),
        "joint_owner": draw_joint_owner(jax.random.fold_in(keys[10], 71), 0),
        "joint_local": touch_ends(jax.random.randint(keys[9], (COMPONENTS, JSLOTS), 0, JOWN), jax.random.fold_in(keys[9], 1), 0, JOWN - 1).astype(jnp.int32),
    }


def component_pass(modes_all, rows_all, item):
    modes, stiff, columns_of, own_flange, flange_to, flange_at, bolt, joint_at = item
    blocks_of = modes.reshape(BROWS, BLOCK, IFACE)
    split_stiff = stiff.reshape(BROWS, BLOCK, NEIGH, BLOCK)
    accum = jnp.zeros((BROWS, BLOCK, IFACE), jnp.float32)
    for column in range(NEIGH):
        taken = blocks_of[columns_of[:, column]].astype(jnp.float32)
        accum = accum + jnp.einsum('rab,rbn->ran', split_stiff[:, :, column, :].astype(jnp.float32), taken)
    product = accum.reshape(ROWS, IFACE)
    entry = jnp.arange(FNODES, dtype=jnp.int32)
    own_rows = own_flange + entry // FN_DEV * ROWS_DEV
    partner_rows = rows_all[flange_to, flange_at] + flange_at // FN_DEV * ROWS_DEV
    partner_vals = modes_all[flange_to, partner_rows].astype(jnp.float32)
    own_vals = modes[own_rows].astype(jnp.float32)
    coupled = product.at[own_rows].add(bolt[:, None] * (own_vals - partner_vals))
    rounded = coupled.astype(jnp.bfloat16)
    reduced = jnp.dot(modes.T, rounded, preferred_element_type=jnp.float32) * (1.0 / math.sqrt(ROWS))
    slots = jnp.arange(JSLOTS, dtype=jnp.int32)
    picked = coupled[joint_at + slots // JS_DEV * ROWS_DEV]
    return (reduced, picked)

def reference(constraint_modes, stiff_blocks, block_cols, flange_rows, flange_dest, flange_match, flange_stiff, joint_rows, joint_owner, joint_local):

    def one_component(item):
        return component_pass(constraint_modes, flange_rows, item)
    reduced_stiff, picked = lax.map(one_component, (constraint_modes, stiff_blocks, block_cols, flange_rows, flange_dest, flange_match, flange_stiff, joint_rows))
    target = (joint_owner * JOWN + joint_local).reshape(-1)
    joint_forces = jnp.zeros((JOINTS, IFACE), jnp.float32).at[target].add(picked.reshape(-1, IFACE))
    return (reduced_stiff, joint_forces)
```

```python
import math

import jax
import jax.numpy as jnp
from jax import lax
from jax.experimental import pallas as pl
from jax.experimental.pallas import tpu as pltpu
from jax.sharding import PartitionSpec as P

MESH = pl.DeviceIdType.MESH
BLOCK = 64
NEIGH = 8
FCAP = 2
JCAP = 4
JOWN = 64
NZ = 8
LANES = 128
f32 = jnp.float32
bf16 = jnp.bfloat16


def iota(shape, dim):
    return lax.broadcasted_iota(jnp.int32, shape, dim).astype(f32)


def ones_where(mask):
    return jnp.where(mask, 1.0, 0.0).astype(bf16)


def dot(left, right):
    return jnp.dot(left, right, preferred_element_type=f32)


def as_column(row):
    n = row.shape[1]
    return jnp.sum(jnp.where(iota((n, n), 0) == iota((n, n), 1), row, 0.0), axis=1, keepdims=True)


def kernel(
    modes_hbm, stiff_hbm, block_cols, flange_rows, flange_dest, flange_match, flange_stiff,
    joint_rows, joint_owner, joint_local,
    reduced_hbm, forces,
    whole, stiff, vec, flange_send, flange_recv, relay, incoming, base, high, low,
    bolt, select_row, joint_select, joint_flange, joint_bolt, joint_base,
    id_send, id_recv, place, rows_send, rows_recv, round_send, round_full,
    part_send, part_recv, reduced,
    load_sem, flange_sem, modes_sem, id_sem, rows_send_sem, rows_recv_sem,
    round_sem, part_send_sem, part_recv_sem, out_sem,
):
    ncomp = lax.axis_size("comp")
    nplane = ncomp // NZ
    comp = lax.axis_index("comp")
    half = lax.axis_index("blk")
    other = 1 - half
    plane = comp // NZ
    zpos = lax.rem(comp, NZ)
    rows, iface = stiff.shape[0], whole.shape[2]
    cols = iface // 2
    nflange = flange_rows.shape[1]
    fslots = ncomp * FCAP
    jslots = ncomp * JCAP
    chunks = iface // LANES
    quarter = chunks // 2
    own_rows = pl.ds(pl.multiple_of(half * rows, rows), rows)
    nblocks = rows // BLOCK
    own_blocks = pl.ds(half * nblocks, nblocks)
    here = half * nplane + plane

    def to(c, b):
        return dict(device_id={"comp": c, "blk": b}, device_id_type=MESH)

    load_modes = pltpu.make_async_copy(modes_hbm, whole.at[own_blocks], load_sem.at[0])
    load_stiff = pltpu.make_async_copy(stiff_hbm.at[0], stiff, load_sem.at[1])
    load_modes.start()
    load_stiff.start()

    barrier = pltpu.get_barrier_semaphore()

    def greet(k, carry):
        pl.semaphore_signal(barrier, inc=1, **to(lax.rem(comp + k, ncomp), half))
        return carry

    def greet_plane(k, carry):
        pl.semaphore_signal(barrier, inc=1, **to(k * NZ + zpos, other))
        return carry

    lax.fori_loop(1, ncomp, greet, 0)
    lax.fori_loop(0, nplane, greet_plane, 0)

    vec[...] = jnp.full(vec.shape, -1.0, f32)
    parity = lax.broadcasted_iota(jnp.int32, (1, nflange), 1) & 1
    vec[0:1, 0:nflange] = flange_rows[...].astype(f32)
    vec[1:2, 0:nflange] = (flange_dest[...] * FCAP + parity).astype(f32)
    vec[2:3, 0:nflange] = (flange_dest[...] * FCAP + (flange_match[...] & 1)).astype(f32)
    vec[3:4, 0:nflange] = flange_stiff[...]
    frow, out_slot, in_slot, fstiff = vec[0:1, :], vec[1:2, :], vec[2:3, :], vec[3:4, :]
    row_of_slot = jnp.sum(
        jnp.where(iota((fslots, LANES), 0) == out_slot, frow + 1.0, 0.0), axis=1, keepdims=True
    ) - 1.0
    pick = ones_where(row_of_slot == iota((fslots, rows), 1))
    load_modes.wait()
    for j in range(0, chunks, 2):
        got = dot(pick, whole[own_blocks, :, j * LANES : (j + 2) * LANES].reshape(rows, 2 * LANES))
        relay[pl.ds(j, fslots, stride=chunks), :] = got[:, :LANES]
        relay[pl.ds(j + 1, fslots, stride=chunks), :] = got[:, LANES:]
    flange_send[...] = relay[...].astype(bf16)
    flange_recv[pl.ds(pl.multiple_of(comp * 16, 16), 16), :] = jnp.zeros((16, LANES), bf16)

    pl.semaphore_wait(barrier, ncomp - 1 + nplane)

    def flange_copy(k):
        dest = lax.rem(comp + k, ncomp)
        return pltpu.make_async_remote_copy(
            flange_send.at[pl.ds(pl.multiple_of(dest * 16, 16), 16)],
            flange_recv.at[pl.ds(pl.multiple_of(comp * 16, 16), 16)],
            flange_sem.at[0], flange_sem.at[1], **to(dest, half),
        )

    def send_flange(k, carry):
        flange_copy(k).start()
        return carry

    lax.fori_loop(1, ncomp, send_flange, 0)

    modes_copy = pltpu.make_async_remote_copy(
        whole.at[own_blocks], whole.at[own_blocks], modes_sem.at[0], modes_sem.at[1], **to(comp, other)
    )
    modes_copy.start()

    owner = joint_owner[...].astype(f32)
    local = joint_local[...].astype(f32)
    njoint = owner.shape[1]
    square = (njoint, njoint)
    before = (as_column(owner) == owner) & (iota(square, 0) < iota(square, 1))
    position = jnp.sum(jnp.where(before, 1.0, 0.0), axis=0, keepdims=True)
    jslot = owner * JCAP + position
    group = NZ * JCAP
    jslot_int = jslot.astype(jnp.int32)
    lane = (jslot_int & (group - 1)) + (plane & 3) * group
    of_plane = ones_where(
        lax.broadcasted_iota(jnp.int32, (nplane, njoint), 0) == (joint_owner[...] // NZ)
    )
    at_lane = jnp.where(
        lax.broadcasted_iota(jnp.int32, (LANES, njoint), 0) == lane, local + 1.0, 0.0
    ).astype(bf16)
    ids = lax.dot_general(of_plane, at_lane, (((1,), (1,)), ((), ())), preferred_element_type=f32)
    for d in range(nplane):
        id_send[d] = ids[d : d + 1, :]
    id_recv[pl.ds(here, 1)] = id_send[pl.ds(plane, 1)]

    def id_copy(k, b):
        dest = lax.rem(plane + k, nplane)
        return pltpu.make_async_remote_copy(
            id_send.at[pl.ds(dest, 1)], id_recv.at[pl.ds(here, 1)],
            id_sem.at[0], id_sem.at[1], **to(dest * NZ + zpos, b),
        )

    def send_ids(k, carry):
        id_copy(k, half).start()
        id_copy(k, other).start()
        return carry

    id_copy(0, other).start()
    lax.fori_loop(1, nplane, send_ids, 0)

    at_row = iota((rows, LANES), 0) == frow
    slot_of_row = jnp.sum(jnp.where(at_row, in_slot + 1.0, 0.0), axis=1, keepdims=True) - 1.0
    bolt[...] = jnp.broadcast_to(
        jnp.sum(jnp.where(at_row, fstiff, 0.0), axis=1, keepdims=True), bolt.shape
    )
    select_row[...] = ones_where(slot_of_row == iota((rows, fslots), 1))
    by_row = as_column(frow) == iota((LANES, rows), 1)
    slots_along = jnp.sum(jnp.where(by_row, as_column(in_slot) + 1.0, 0.0), axis=0, keepdims=True)
    bolts_along = jnp.sum(jnp.where(by_row, as_column(fstiff), 0.0), axis=0, keepdims=True)
    joint_row = jnp.sum(
        jnp.where(iota((jslots, njoint), 0) == jslot, joint_rows[...].astype(f32) + 1.0, 0.0),
        axis=1, keepdims=True,
    ) - 1.0
    takes = joint_row == iota((jslots, rows), 1)
    joint_select[...] = ones_where(takes)
    joint_slot = jnp.sum(jnp.where(takes, slots_along, 0.0), axis=1, keepdims=True) - 1.0
    joint_flange[...] = ones_where(joint_slot == iota((jslots, fslots), 1))
    joint_bolt[...] = jnp.broadcast_to(
        jnp.sum(jnp.where(takes, bolts_along, 0.0), axis=1, keepdims=True), joint_bolt.shape
    )

    load_stiff.wait()
    modes_copy.wait()

    def block_row(r, carry):
        at = pl.ds(pl.multiple_of(r * BLOCK, BLOCK), BLOCK)
        taken = jnp.concatenate(
            [
                whole[block_cols[0, r, k]]
                for k in range(NEIGH)
            ],
            axis=0,
        )
        own = whole[half * nblocks + r].astype(f32)
        value = dot(stiff[at, :], taken) + bolt[at, 0:1] * own
        top = value.astype(bf16)
        rest = (value - top.astype(f32)).astype(bf16)
        for e in range(2):
            here_cols = slice(e * cols, (e + 1) * cols)
            base[e, at, :] = value[:, here_cols]
            high[e, at, :] = top[:, here_cols]
            low[e, at, :] = rest[:, here_cols]
        return carry

    lax.fori_loop(0, rows // BLOCK, block_row, 0)
    for e in range(2):
        joint_base[e] = dot(joint_select[...], high[e]) + dot(joint_select[...], low[e])

    id_all = id_recv.at[pl.ds(0, 2 * nplane - 1)]
    id_wait = pltpu.make_async_remote_copy(
        id_all, id_all, id_sem.at[0], id_sem.at[1], **to(comp, other)
    )
    id_wait.wait_recv()
    lane_z = ((lax.broadcasted_iota(jnp.int32, (1, LANES), 1) & (group - 1)) // JCAP).astype(f32)
    for g in range(2 * nplane // 4):
        four = id_recv[4 * g] + id_recv[4 * g + 1] + id_recv[4 * g + 2] + id_recv[4 * g + 3]
        key = jnp.where(four > 0.5, lane_z * JOWN + four - 1.0, -1.0)
        place[:, g * LANES : (g + 1) * LANES] = ones_where(iota((NZ * JOWN, LANES), 0) == key)

    sent = pl.ds(0, (ncomp - 1) * 16)
    flange_wait = pltpu.make_async_remote_copy(
        flange_send.at[sent], flange_recv.at[sent], flange_sem.at[0], flange_sem.at[1],
        **to(comp, other),
    )
    flange_wait.wait_recv()
    relay[...] = flange_recv[...].astype(f32)

    def rows_copy(k, e, jj, b):
        dest = lax.rem(plane + k, nplane)
        return pltpu.make_async_remote_copy(
            rows_send.at[e * quarter + jj, pl.ds(pl.multiple_of(dest * group, group), group)],
            rows_recv.at[jj, pl.ds(pl.multiple_of(here * group, group), group)],
            rows_send_sem, rows_recv_sem.at[jj], **to(dest * NZ + zpos, b),
        )

    for jj in range(quarter):
        for e in range(2):
            j = e * quarter + jj
            part = relay[pl.ds(j, fslots, stride=chunks), :].astype(bf16)
            span = slice(jj * LANES, (jj + 1) * LANES)
            incoming[e, :, span] = part
            rows_send[j] = (
                joint_base[e, :, span] - joint_bolt[...] * dot(joint_flange[...], part)
            ).astype(bf16)

            def send_rows(k, carry, e=e, jj=jj):
                rows_copy(k, e, jj, jnp.int32(e)).start()
                return carry

            lax.fori_loop(1, nplane, send_rows, 0)

            @pl.when(half != e)
            def _(e=e, jj=jj):
                rows_copy(0, e, jj, jnp.int32(e)).start()

            @pl.when(half == e)
            def _(jj=jj, j=j):
                rows_recv[jj, pl.ds(pl.multiple_of(here * group, group), group), :] = rows_send[
                    j, pl.ds(pl.multiple_of(plane * group, group), group), :
                ]

    step = 256

    def round_rows(which, m):
        at = pl.ds(pl.multiple_of(m * step, step), step)
        partner = dot(select_row[at, :], incoming[which])
        return (base[which, at, :] - bolt[at, 0:1] * partner).astype(bf16)

    def round_other(m, carry):
        round_send[pl.ds(pl.multiple_of(m * step, step), step), :] = round_rows(other, m)
        return carry

    def round_own(m, carry):
        at = pl.ds(pl.multiple_of(half * rows + m * step, step), step)
        round_full[at, :] = round_rows(half, m)
        return carry

    lax.fori_loop(0, rows // step, round_other, 0)
    round_copy = pltpu.make_async_remote_copy(
        round_send, round_full.at[own_rows], round_sem.at[0], round_sem.at[1], **to(comp, other)
    )
    round_copy.start()
    lax.fori_loop(0, rows // step, round_own, 0)

    factor = 1.0 / math.sqrt(2 * rows)
    got_rows = pl.ds(0, (2 * nplane - 1) * group)
    width = iface // quarter
    copies_out = []
    for jj in range(quarter):
        landed = rows_recv.at[jj, got_rows]
        pltpu.make_async_remote_copy(
            landed, landed, rows_send_sem, rows_recv_sem.at[jj], **to(comp, other)
        ).wait_recv()
        part_send[jj] = dot(place[...], rows_recv[jj]).astype(bf16)
        mine = pl.ds(pl.multiple_of(zpos * JOWN, JOWN), JOWN)
        part_recv[jj, mine, :] = part_send[jj, mine, :]

        def send_part(k, carry, jj=jj):
            dest = lax.rem(zpos + k, NZ)
            pltpu.make_async_remote_copy(
                part_send.at[jj, pl.ds(pl.multiple_of(dest * JOWN, JOWN), JOWN)],
                part_recv.at[jj, pl.ds(pl.multiple_of(zpos * JOWN, JOWN), JOWN)],
                part_send_sem, part_recv_sem.at[jj], **to(plane * NZ + dest, half),
            ).start()
            return carry

        lax.fori_loop(1, NZ, send_part, 0)
        if jj == 0:
            round_copy.wait()
        span = slice(jj * width, (jj + 1) * width)
        reduced[span, :] = (
            lax.dot_general(
                whole[:, :, span].reshape(2 * rows, width), round_full[...], (((0,), (0,)), ((), ())),
                preferred_element_type=f32,
            )
            * factor
        )
        copy_out = pltpu.make_async_copy(
            reduced.at[span], reduced_hbm.at[0, span], out_sem.at[jj]
        )
        copy_out.start()
        copies_out.append(copy_out)

    for jj in range(quarter):
        landed = part_recv.at[jj, pl.ds(0, (NZ - 1) * JOWN)]
        pltpu.make_async_remote_copy(
            landed, landed, part_send_sem, part_recv_sem.at[jj], **to(comp, other)
        ).wait_recv()
        total = part_recv[jj, 0:JOWN, :].astype(f32)
        for z in range(1, NZ):
            total = total + part_recv[jj, z * JOWN : (z + 1) * JOWN, :].astype(f32)
        forces[:, jj * LANES : (jj + 1) * LANES] = total

    flange_wait.wait_send()
    id_wait.wait_send()

    for jj in range(quarter):
        gone = rows_recv.at[jj, got_rows]
        pltpu.make_async_remote_copy(
            gone, gone, rows_send_sem, rows_recv_sem.at[jj], **to(comp, other)
        ).wait_send()
        gone = part_recv.at[jj, pl.ds(0, (NZ - 1) * JOWN)]
        pltpu.make_async_remote_copy(
            gone, gone, part_send_sem, part_recv_sem.at[jj], **to(comp, other)
        ).wait_send()
    for copy_out in copies_out:
        copy_out.wait()


def body(*args):
    modes, stiff = args[0], args[1]
    ncomp = lax.axis_size("comp")
    rows, iface = modes.shape[1:]
    cols = iface // 2
    quarter = cols // LANES
    width = stiff.shape[2]
    fslots, jslots = ncomp * FCAP, ncomp * JCAP
    nplane = ncomp // NZ
    dma = pltpu.SemaphoreType.DMA
    vmem = pl.BlockSpec(memory_space=pltpu.VMEM)
    hbm = pl.BlockSpec(memory_space=pl.ANY)
    scratch = [
        pltpu.VMEM((2 * rows // BLOCK, BLOCK, iface), bf16),
        pltpu.VMEM((rows, width), bf16),
        pltpu.VMEM((8, LANES), f32),
        pltpu.VMEM((ncomp * 16, LANES), bf16),
        pltpu.VMEM((ncomp * 16, LANES), bf16),
        pltpu.VMEM((ncomp * 16, LANES), f32),
        pltpu.VMEM((2, fslots, cols), bf16),
        pltpu.VMEM((2, rows, cols), f32),
        pltpu.VMEM((2, rows, cols), bf16),
        pltpu.VMEM((2, rows, cols), bf16),
        pltpu.VMEM((rows, LANES), f32),
        pltpu.VMEM((rows, fslots), bf16),
        pltpu.VMEM((jslots, rows), bf16),
        pltpu.VMEM((jslots, fslots), bf16),
        pltpu.VMEM((jslots, LANES), f32),
        pltpu.VMEM((2, jslots, cols), f32),
        pltpu.VMEM((nplane, 1, LANES), f32),
        pltpu.VMEM((2 * nplane, 1, LANES), f32),
        pltpu.VMEM((NZ * JOWN, 2 * nplane * NZ * JCAP), bf16),
        pltpu.VMEM((2 * quarter, jslots, LANES), bf16),
        pltpu.VMEM((quarter, 2 * jslots, LANES), bf16),
        pltpu.VMEM((rows, cols), bf16),
        pltpu.VMEM((2 * rows, cols), bf16),
        pltpu.VMEM((quarter, NZ * JOWN, LANES), bf16),
        pltpu.VMEM((quarter, NZ * JOWN, LANES), bf16),
        pltpu.VMEM((iface, cols), f32),
        dma((2,)), dma((2,)), dma((2,)), dma((2,)), dma, dma((quarter,)),
        dma((2,)), dma, dma((quarter,)), dma((quarter,)),
    ]
    return pl.pallas_call(
        kernel,
        out_shape=(
            jax.ShapeDtypeStruct((1, iface, cols), f32),
            jax.ShapeDtypeStruct((JOWN, cols), f32),
        ),
        in_specs=[hbm, hbm, pl.BlockSpec(memory_space=pltpu.SMEM)] + [vmem] * 7,
        out_specs=(hbm, vmem),
        scratch_shapes=scratch,
        compiler_params=pltpu.CompilerParams(
            collective_id=0, has_side_effects=True, vmem_limit_bytes=56 << 20
        ),
    )(modes.reshape(rows // BLOCK, BLOCK, iface), *args[1:])


def solution(mesh):
    placed = (
        P("comp", "blk", None),
        P("comp", "blk", None),
        P("comp", "blk", None),
        P("comp", "blk"),
        P("comp", "blk"),
        P("comp", "blk"),
        P("comp", "blk"),
        P("comp", "blk"),
        P("comp", "blk"),
        P("comp", "blk"),
    )
    return jax.shard_map(
        body,
        mesh=mesh,
        in_specs=placed,
        out_specs=(P("comp", None, "blk"), P("comp", "blk")),
        check_vma=False,
    )
```

```python
import math

import jax
import jax.numpy as jnp
from jax import lax
from jax.experimental import pallas as pl
from jax.experimental.pallas import tpu as pltpu
from jax.sharding import PartitionSpec as P

MESH = pl.DeviceIdType.MESH
BLOCK = 64
NEIGH = 8
FCAP = 2
JCAP = 4
JOWN = 64
NZ = 8
LANES = 128
f32 = jnp.float32
bf16 = jnp.bfloat16


def iota(shape, dim):
    return lax.broadcasted_iota(jnp.int32, shape, dim).astype(f32)


def ones_where(mask):
    return jnp.where(mask, 1.0, 0.0).astype(bf16)


def dot(left, right):
    return jnp.dot(left, right, preferred_element_type=f32)


def as_column(row):
    n = row.shape[1]
    return jnp.sum(jnp.where(iota((n, n), 0) == iota((n, n), 1), row, 0.0), axis=1, keepdims=True)


def kernel(
    modes_hbm, stiff_hbm, block_cols, flange_rows, flange_dest, flange_match, flange_stiff,
    joint_rows, joint_owner, joint_local,
    reduced, forces,
    whole, stiff, vec, over_plane, plane_recv, regroup, over_z, z_recv, incoming, base, high, low,
    bolt, select_row, joint_select, joint_flange, joint_bolt, joint_base,
    id_send, id_recv, place, rows_send, rows_recv, round_send, round_full,
    part_send, part_recv,
    load_sem, plane_sem, plane_recv_sem, z_sem, z_recv_sem, modes_sem, id_sem, rows_send_sem, rows_recv_sem,
    round_sem, part_send_sem, part_recv_sem,
):
    ncomp = lax.axis_size("comp")
    nplane = ncomp // NZ
    comp = lax.axis_index("comp")
    half = lax.axis_index("blk")
    other = 1 - half
    plane = comp // NZ
    zpos = lax.rem(comp, NZ)
    rows, iface = stiff.shape[0], whole.shape[2]
    cols = iface // 2
    nflange = flange_rows.shape[1]
    fslots = ncomp * FCAP
    jslots = ncomp * JCAP
    chunks = iface // LANES
    quarter = chunks // 2
    own_rows = pl.ds(pl.multiple_of(half * rows, rows), rows)
    nblocks = rows // BLOCK
    own_blocks = pl.ds(half * nblocks, nblocks)
    here = half * nplane + plane

    def to(c, b):
        return dict(device_id={"comp": c, "blk": b}, device_id_type=MESH)

    load_modes = pltpu.make_async_copy(modes_hbm, whole.at[own_blocks], load_sem.at[0])
    load_stiff = pltpu.make_async_copy(stiff_hbm.at[0], stiff, load_sem.at[1])
    load_modes.start()
    load_stiff.start()

    barrier = pltpu.get_barrier_semaphore()

    def greet_z(k, carry):
        pl.semaphore_signal(barrier, inc=1, **to(plane * NZ + lax.rem(zpos + k, NZ), half))
        return carry

    def greet_plane(k, carry):
        there = lax.rem(plane + k, nplane) * NZ + zpos
        pl.semaphore_signal(barrier, inc=1, **to(there, other))
        pl.semaphore_signal(barrier, inc=1, **to(there, half))
        return carry

    lax.fori_loop(1, NZ, greet_z, 0)
    lax.fori_loop(1, nplane, greet_plane, 0)
    pl.semaphore_signal(barrier, inc=1, **to(comp, other))

    vec[...] = jnp.full(vec.shape, -1.0, f32)
    parity = lax.broadcasted_iota(jnp.int32, (1, nflange), 1) & 1
    vec[0:1, 0:nflange] = flange_rows[...].astype(f32)
    vec[1:2, 0:nflange] = (flange_dest[...] * FCAP + parity).astype(f32)
    vec[2:3, 0:nflange] = (
        ((flange_dest[...] & (NZ - 1)) * nplane + flange_dest[...] // NZ) * FCAP
        + (flange_match[...] & 1)
    ).astype(f32)
    vec[3:4, 0:nflange] = flange_stiff[...]
    frow, out_slot, in_slot, fstiff = vec[0:1, :], vec[1:2, :], vec[2:3, :], vec[3:4, :]
    row_of_slot = jnp.sum(
        jnp.where(iota((fslots, LANES), 0) == out_slot, frow + 1.0, 0.0), axis=1, keepdims=True
    ) - 1.0
    pick = ones_where(row_of_slot == iota((fslots, rows), 1))
    load_modes.wait()
    pair = NZ * FCAP
    line = nplane * FCAP
    in_plane = pl.ds(pl.multiple_of(plane * pair, pair), pair)
    in_line = pl.ds(pl.multiple_of(zpos * line, line), line)
    order = [e * quarter + jj for jj in range(quarter) for e in range(2)]

    def gather(j):
        got = dot(pick, whole[own_blocks, :, j * LANES : (j + 2) * LANES].reshape(rows, 2 * LANES))
        for i in range(2):
            over_plane[j + i] = got[:, i * LANES : (i + 1) * LANES].astype(bf16)
            plane_recv[j + i, in_plane, :] = over_plane[j + i, in_plane, :]

    def send_over_plane(j):
        def send(k, carry):
            dest = lax.rem(plane + k, nplane)
            pltpu.make_async_remote_copy(
                over_plane.at[j, pl.ds(pl.multiple_of(dest * pair, pair), pair)],
                plane_recv.at[j, in_plane],
                plane_sem, plane_recv_sem.at[j], **to(dest * NZ + zpos, half),
            ).start()
            return carry

        lax.fori_loop(1, nplane, send, 0)

    for j in range(0, chunks, 2):
        gather(j)

    pl.semaphore_wait(barrier, NZ - 1 + 2 * nplane - 1)
    modes_copy = pltpu.make_async_remote_copy(
        whole.at[own_blocks], whole.at[own_blocks], modes_sem.at[0], modes_sem.at[1], **to(comp, other)
    )
    modes_copy.start()
    for j in order:
        send_over_plane(j)

    turn = lax.broadcasted_iota(jnp.int32, (fslots, fslots), 0)
    turned = ((turn // FCAP) & (nplane - 1)) * pair + turn // line * FCAP + (turn & (FCAP - 1))
    regroup[...] = ones_where(turned == lax.broadcasted_iota(jnp.int32, (fslots, fslots), 1))

    def plane_wait(j):
        landed = plane_recv.at[j, pl.ds(0, (nplane - 1) * pair)]
        return pltpu.make_async_remote_copy(
            landed, landed, plane_sem, plane_recv_sem.at[j], **to(comp, other)
        )

    def z_wait(j):
        landed = z_recv.at[j, pl.ds(0, (NZ - 1) * line)]
        return pltpu.make_async_remote_copy(
            landed, landed, z_sem, z_recv_sem.at[j], **to(comp, other)
        )

    def pass_on(j):
        plane_wait(j).wait_recv()
        over_z[j] = dot(regroup[...], plane_recv[j]).astype(bf16)
        z_recv[j, in_line, :] = over_z[j, in_line, :]

        def send(k, carry):
            dest = lax.rem(zpos + k, NZ)
            pltpu.make_async_remote_copy(
                over_z.at[j, pl.ds(pl.multiple_of(dest * line, line), line)],
                z_recv.at[j, in_line],
                z_sem, z_recv_sem.at[j], **to(plane * NZ + dest, half),
            ).start()
            return carry

        lax.fori_loop(1, NZ, send, 0)

    owner = joint_owner[...].astype(f32)
    local = joint_local[...].astype(f32)
    njoint = owner.shape[1]
    square = (njoint, njoint)
    before = (as_column(owner) == owner) & (iota(square, 0) < iota(square, 1))
    position = jnp.sum(jnp.where(before, 1.0, 0.0), axis=0, keepdims=True)
    jslot = owner * JCAP + position
    group = NZ * JCAP
    jslot_int = jslot.astype(jnp.int32)
    lane = (jslot_int & (group - 1)) + (plane & 3) * group
    of_plane = ones_where(
        lax.broadcasted_iota(jnp.int32, (nplane, njoint), 0) == (joint_owner[...] // NZ)
    )
    at_lane = jnp.where(
        lax.broadcasted_iota(jnp.int32, (LANES, njoint), 0) == lane, local + 1.0, 0.0
    ).astype(bf16)
    ids = lax.dot_general(of_plane, at_lane, (((1,), (1,)), ((), ())), preferred_element_type=f32)
    for d in range(nplane):
        id_send[d] = ids[d : d + 1, :]
    id_recv[pl.ds(here, 1)] = id_send[pl.ds(plane, 1)]

    def id_copy(k, b):
        dest = lax.rem(plane + k, nplane)
        return pltpu.make_async_remote_copy(
            id_send.at[pl.ds(dest, 1)], id_recv.at[pl.ds(here, 1)],
            id_sem.at[0], id_sem.at[1], **to(dest * NZ + zpos, b),
        )

    def send_ids(k, carry):
        id_copy(k, half).start()
        id_copy(k, other).start()
        return carry

    id_copy(0, other).start()
    lax.fori_loop(1, nplane, send_ids, 0)

    pass_on(order[0])

    at_row = iota((rows, LANES), 0) == frow
    slot_of_row = jnp.sum(jnp.where(at_row, in_slot + 1.0, 0.0), axis=1, keepdims=True) - 1.0
    bolt[...] = jnp.broadcast_to(
        jnp.sum(jnp.where(at_row, fstiff, 0.0), axis=1, keepdims=True), bolt.shape
    )
    select_row[...] = ones_where(slot_of_row == iota((rows, fslots), 1))
    by_row = as_column(frow) == iota((LANES, rows), 1)
    slots_along = jnp.sum(jnp.where(by_row, as_column(in_slot) + 1.0, 0.0), axis=0, keepdims=True)
    bolts_along = jnp.sum(jnp.where(by_row, as_column(fstiff), 0.0), axis=0, keepdims=True)
    joint_row = jnp.sum(
        jnp.where(iota((jslots, njoint), 0) == jslot, joint_rows[...].astype(f32) + 1.0, 0.0),
        axis=1, keepdims=True,
    ) - 1.0
    takes = joint_row == iota((jslots, rows), 1)
    joint_select[...] = ones_where(takes)
    joint_slot = jnp.sum(jnp.where(takes, slots_along, 0.0), axis=1, keepdims=True) - 1.0
    joint_flange[...] = ones_where(joint_slot == iota((jslots, fslots), 1))
    joint_bolt[...] = jnp.broadcast_to(
        jnp.sum(jnp.where(takes, bolts_along, 0.0), axis=1, keepdims=True), joint_bolt.shape
    )

    pass_on(order[1])

    load_stiff.wait()
    modes_copy.wait()

    def block_row(r, carry):
        at = pl.ds(pl.multiple_of(r * BLOCK, BLOCK), BLOCK)
        taken = jnp.concatenate(
            [
                whole[block_cols[0, k, r]]
                for k in range(NEIGH)
            ],
            axis=0,
        )
        own = whole[half * nblocks + r].astype(f32)
        value = dot(stiff[at, :], taken) + bolt[at, 0:1] * own
        top = value.astype(bf16)
        rest = (value - top.astype(f32)).astype(bf16)
        for e in range(2):
            here_cols = slice(e * cols, (e + 1) * cols)
            base[e, at, :] = value[:, here_cols]
            high[e, at, :] = top[:, here_cols]
            low[e, at, :] = rest[:, here_cols]
        return carry

    pieces = 3
    at_piece = [p * nblocks // pieces for p in range(pieces + 1)]
    for p in range(pieces):
        lax.fori_loop(at_piece[p], at_piece[p + 1], block_row, 0)
        pass_on(order[2 + 2 * p])
        pass_on(order[3 + 2 * p])

    id_all = id_recv.at[pl.ds(0, 2 * nplane - 1)]
    id_wait = pltpu.make_async_remote_copy(
        id_all, id_all, id_sem.at[0], id_sem.at[1], **to(comp, other)
    )
    id_wait.wait_recv()
    lane_z = ((lax.broadcasted_iota(jnp.int32, (1, LANES), 1) & (group - 1)) // JCAP).astype(f32)
    for g in range(2 * nplane // 4):
        four = id_recv[4 * g] + id_recv[4 * g + 1] + id_recv[4 * g + 2] + id_recv[4 * g + 3]
        key = jnp.where(four > 0.5, lane_z * JOWN + four - 1.0, -1.0)
        place[:, g * LANES : (g + 1) * LANES] = ones_where(iota((NZ * JOWN, LANES), 0) == key)

    def rows_copy(k, e, jj, b):
        dest = lax.rem(plane + k, nplane)
        return pltpu.make_async_remote_copy(
            rows_send.at[e * quarter + jj, pl.ds(pl.multiple_of(dest * group, group), group)],
            rows_recv.at[jj, pl.ds(pl.multiple_of(here * group, group), group)],
            rows_send_sem, rows_recv_sem.at[jj], **to(dest * NZ + zpos, b),
        )

    for jj in range(quarter):
        for e in range(2):
            j = e * quarter + jj
            if jj % 2 == 0:
                two = slice(jj * LANES, (jj + 2) * LANES)
                joint_base[e, :, two] = dot(joint_select[...], high[e, :, two]) + dot(
                    joint_select[...], low[e, :, two]
                )
            z_wait(j).wait_recv()
            part = z_recv[j]
            span = slice(jj * LANES, (jj + 1) * LANES)
            incoming[e, :, span] = part
            rows_send[j] = (
                joint_base[e, :, span] - joint_bolt[...] * dot(joint_flange[...], part)
            ).astype(bf16)

            def send_rows(k, carry, e=e, jj=jj):
                rows_copy(k, e, jj, jnp.int32(e)).start()
                return carry

            lax.fori_loop(1, nplane, send_rows, 0)

            @pl.when(half != e)
            def _(e=e, jj=jj):
                rows_copy(0, e, jj, jnp.int32(e)).start()

            @pl.when(half == e)
            def _(jj=jj, j=j):
                rows_recv[jj, pl.ds(pl.multiple_of(here * group, group), group), :] = rows_send[
                    j, pl.ds(pl.multiple_of(plane * group, group), group), :
                ]

    step = 256

    def round_rows(which, m):
        at = pl.ds(pl.multiple_of(m * step, step), step)
        partner = dot(select_row[at, :], incoming[which])
        return (base[which, at, :] - bolt[at, 0:1] * partner).astype(bf16)

    def round_other(m, carry):
        round_send[pl.ds(pl.multiple_of(m * step, step), step), :] = round_rows(other, m)
        return carry

    def round_own(m, carry):
        at = pl.ds(pl.multiple_of(half * rows + m * step, step), step)
        round_full[at, :] = round_rows(half, m)
        return carry

    lax.fori_loop(0, rows // step, round_other, 0)
    round_copy = pltpu.make_async_remote_copy(
        round_send, round_full.at[own_rows], round_sem.at[0], round_sem.at[1], **to(comp, other)
    )
    round_copy.start()
    lax.fori_loop(0, rows // step, round_own, 0)

    factor = 1.0 / math.sqrt(2 * rows)
    got_rows = pl.ds(0, (2 * nplane - 1) * group)
    width = iface // quarter
    for jj in range(quarter):
        landed = rows_recv.at[jj, got_rows]
        pltpu.make_async_remote_copy(
            landed, landed, rows_send_sem, rows_recv_sem.at[jj], **to(comp, other)
        ).wait_recv()
        part_send[jj] = dot(place[...], rows_recv[jj]).astype(bf16)
        mine = pl.ds(pl.multiple_of(zpos * JOWN, JOWN), JOWN)
        part_recv[jj, mine, :] = part_send[jj, mine, :]

        def send_part(k, carry, jj=jj):
            dest = lax.rem(zpos + k, NZ)
            pltpu.make_async_remote_copy(
                part_send.at[jj, pl.ds(pl.multiple_of(dest * JOWN, JOWN), JOWN)],
                part_recv.at[jj, pl.ds(pl.multiple_of(zpos * JOWN, JOWN), JOWN)],
                part_send_sem, part_recv_sem.at[jj], **to(plane * NZ + dest, half),
            ).start()
            return carry

        lax.fori_loop(1, NZ, send_part, 0)
        if jj == 0:
            round_copy.wait()
        span = slice(jj * width, (jj + 1) * width)
        reduced[0, span, :] = (
            lax.dot_general(
                whole[:, :, span].reshape(2 * rows, width), round_full[...], (((0,), (0,)), ((), ())),
                preferred_element_type=f32,
            )
            * factor
        )

    for jj in range(quarter):
        landed = part_recv.at[jj, pl.ds(0, (NZ - 1) * JOWN)]
        pltpu.make_async_remote_copy(
            landed, landed, part_send_sem, part_recv_sem.at[jj], **to(comp, other)
        ).wait_recv()
        total = part_recv[jj, 0:JOWN, :].astype(f32)
        for z in range(1, NZ):
            total = total + part_recv[jj, z * JOWN : (z + 1) * JOWN, :].astype(f32)
        forces[:, jj * LANES : (jj + 1) * LANES] = total

    for j in order:
        plane_wait(j).wait_send()
        z_wait(j).wait_send()
    id_wait.wait_send()

    for jj in range(quarter):
        gone = rows_recv.at[jj, got_rows]
        pltpu.make_async_remote_copy(
            gone, gone, rows_send_sem, rows_recv_sem.at[jj], **to(comp, other)
        ).wait_send()
        gone = part_recv.at[jj, pl.ds(0, (NZ - 1) * JOWN)]
        pltpu.make_async_remote_copy(
            gone, gone, part_send_sem, part_recv_sem.at[jj], **to(comp, other)
        ).wait_send()


def body(*args):
    modes, stiff = args[0], args[1]
    ncomp = lax.axis_size("comp")
    rows, iface = modes.shape[1:]
    cols = iface // 2
    quarter = cols // LANES
    chunks = 2 * quarter
    width = stiff.shape[2]
    fslots, jslots = ncomp * FCAP, ncomp * JCAP
    nplane = ncomp // NZ
    dma = pltpu.SemaphoreType.DMA
    vmem = pl.BlockSpec(memory_space=pltpu.VMEM)
    hbm = pl.BlockSpec(memory_space=pl.ANY)
    scratch = [
        pltpu.VMEM((2 * rows // BLOCK, BLOCK, iface), bf16),
        pltpu.VMEM((rows, width), bf16),
        pltpu.VMEM((8, LANES), f32),
        pltpu.VMEM((chunks, fslots, LANES), bf16),
        pltpu.VMEM((chunks, fslots, LANES), bf16),
        pltpu.VMEM((fslots, fslots), bf16),
        pltpu.VMEM((chunks, fslots, LANES), bf16),
        pltpu.VMEM((chunks, fslots, LANES), bf16),
        pltpu.VMEM((2, fslots, cols), bf16),
        pltpu.VMEM((2, rows, cols), f32),
        pltpu.VMEM((2, rows, cols), bf16),
        pltpu.VMEM((2, rows, cols), bf16),
        pltpu.VMEM((rows, LANES), f32),
        pltpu.VMEM((rows, fslots), bf16),
        pltpu.VMEM((jslots, rows), bf16),
        pltpu.VMEM((jslots, fslots), bf16),
        pltpu.VMEM((jslots, LANES), f32),
        pltpu.VMEM((2, jslots, cols), f32),
        pltpu.VMEM((nplane, 1, LANES), f32),
        pltpu.VMEM((2 * nplane, 1, LANES), f32),
        pltpu.VMEM((NZ * JOWN, 2 * nplane * NZ * JCAP), bf16),
        pltpu.VMEM((2 * quarter, jslots, LANES), bf16),
        pltpu.VMEM((quarter, 2 * jslots, LANES), bf16),
        pltpu.VMEM((rows, cols), bf16),
        pltpu.VMEM((2 * rows, cols), bf16),
        pltpu.VMEM((quarter, NZ * JOWN, LANES), bf16),
        pltpu.VMEM((quarter, NZ * JOWN, LANES), bf16),
        dma((2,)), dma, dma((chunks,)), dma, dma((chunks,)),
        dma((2,)), dma((2,)), dma, dma((quarter,)),
        dma((2,)), dma, dma((quarter,)),
    ]
    return pl.pallas_call(
        kernel,
        out_shape=(
            pltpu.VMEM((1, iface, cols), f32),
            pltpu.VMEM((JOWN, cols), f32),
        ),
        in_specs=[hbm, hbm, pl.BlockSpec(memory_space=pltpu.SMEM)] + [vmem] * 7,
        out_specs=(vmem, vmem),
        scratch_shapes=scratch,
        compiler_params=pltpu.CompilerParams(
            collective_id=0, has_side_effects=True, vmem_limit_bytes=56 << 20
        ),
    )(modes.reshape(rows // BLOCK, BLOCK, iface), stiff, jnp.swapaxes(args[2], 1, 2), *args[3:])


def solution(mesh):
    placed = (
        P("comp", "blk", None),
        P("comp", "blk", None),
        P("comp", "blk", None),
        P("comp", "blk"),
        P("comp", "blk"),
        P("comp", "blk"),
        P("comp", "blk"),
        P("comp", "blk"),
        P("comp", "blk"),
        P("comp", "blk"),
    )
    return jax.shard_map(
        body,
        mesh=mesh,
        in_specs=placed,
        out_specs=(P("comp", None, "blk"), P("comp", "blk")),
        check_vma=False,
    )
```

```python
import math

import jax
import jax.numpy as jnp
from jax import lax
from jax.experimental import pallas as pl
from jax.experimental.pallas import tpu as pltpu
from jax.sharding import PartitionSpec as P

MESH = pl.DeviceIdType.MESH
BLOCK = 64
NEIGH = 8
FCAP = 2
JCAP = 4
JOWN = 64
NZ = 8
LANES = 128
f32 = jnp.float32
bf16 = jnp.bfloat16


def iota(shape, dim):
    return lax.broadcasted_iota(jnp.int32, shape, dim).astype(f32)


def ones_where(mask):
    return jnp.where(mask, 1.0, 0.0).astype(bf16)


def dot(left, right):
    return jnp.dot(left, right, preferred_element_type=f32)


def as_column(row):
    n = row.shape[1]
    return jnp.sum(jnp.where(iota((n, n), 0) == iota((n, n), 1), row, 0.0), axis=1, keepdims=True)


def kernel(
    modes_hbm, stiff_hbm, block_cols_hbm, flange_rows_hbm, flange_dest_hbm, flange_match_hbm,
    flange_stiff_hbm, joint_rows_hbm, joint_owner_hbm, joint_local_hbm,
    reduced, forces,
    block_cols, flange_rows, flange_dest, flange_match, flange_stiff,
    joint_rows, joint_owner, joint_local,
    whole, stiff, vec, over_plane, plane_recv, regroup, over_z, z_recv, incoming, base, high, low,
    bolt, select_row, joint_select, joint_flange, joint_bolt, joint_base,
    id_send, id_recv, place, rows_send, rows_recv, round_send, round_full,
    part_send, part_recv,
    load_sem, small_sem, plane_sem, plane_recv_sem, z_sem, z_recv_sem, modes_sem, id_sem, rows_send_sem, rows_recv_sem,
    round_sem, part_send_sem, part_recv_sem,
):
    ncomp = lax.axis_size("comp")
    nplane = ncomp // NZ
    comp = lax.axis_index("comp")
    half = lax.axis_index("blk")
    other = 1 - half
    plane = comp // NZ
    zpos = lax.rem(comp, NZ)
    rows, iface = stiff.shape[0], whole.shape[2]
    cols = iface // 2
    nflange = flange_rows.shape[1]
    fslots = ncomp * FCAP
    jslots = ncomp * JCAP
    chunks = iface // LANES
    quarter = chunks // 2
    own_rows = pl.ds(pl.multiple_of(half * rows, rows), rows)
    nblocks = rows // BLOCK
    own_blocks = pl.ds(half * nblocks, nblocks)
    here = half * nplane + plane

    def to(c, b):
        return dict(device_id={"comp": c, "blk": b}, device_id_type=MESH)

    load_modes = pltpu.make_async_copy(modes_hbm, whole.at[own_blocks], load_sem.at[0])
    load_stiff = pltpu.make_async_copy(stiff_hbm.at[0], stiff, load_sem.at[1])
    loads = [
        pltpu.make_async_copy(source, target, small_sem.at[i])
        for i, (source, target) in enumerate(
            (
                (flange_rows_hbm, flange_rows),
                (flange_dest_hbm, flange_dest),
                (flange_match_hbm, flange_match),
                (flange_stiff_hbm, flange_stiff),
                (joint_rows_hbm, joint_rows),
                (joint_owner_hbm, joint_owner),
                (joint_local_hbm, joint_local),
                (block_cols_hbm, block_cols),
            )
        )
    ]
    for load in loads[:4]:
        load.start()
    load_modes.start()
    for load in loads[4:]:
        load.start()
    load_stiff.start()

    barrier = pltpu.get_barrier_semaphore()

    def greet_z(k, carry):
        pl.semaphore_signal(barrier, inc=1, **to(plane * NZ + lax.rem(zpos + k, NZ), half))
        return carry

    def greet_plane(k, carry):
        there = lax.rem(plane + k, nplane) * NZ + zpos
        pl.semaphore_signal(barrier, inc=1, **to(there, other))
        pl.semaphore_signal(barrier, inc=1, **to(there, half))
        return carry

    lax.fori_loop(1, NZ, greet_z, 0, unroll=7)
    lax.fori_loop(1, nplane, greet_plane, 0, unroll=5)
    pl.semaphore_signal(barrier, inc=1, **to(comp, other))

    for load in loads[:4]:
        load.wait()
    vec[...] = jnp.full(vec.shape, -1.0, f32)
    parity = lax.broadcasted_iota(jnp.int32, (1, nflange), 1) & 1
    vec[0:1, 0:nflange] = flange_rows[...].astype(f32)
    vec[1:2, 0:nflange] = (flange_dest[...] * FCAP + parity).astype(f32)
    vec[2:3, 0:nflange] = (
        ((flange_dest[...] & (NZ - 1)) * nplane + flange_dest[...] // NZ) * FCAP
        + (flange_match[...] & 1)
    ).astype(f32)
    vec[3:4, 0:nflange] = flange_stiff[...]
    frow, out_slot, in_slot, fstiff = vec[0:1, :], vec[1:2, :], vec[2:3, :], vec[3:4, :]
    row_of_slot = jnp.sum(
        jnp.where(iota((fslots, LANES), 0) == out_slot, frow + 1.0, 0.0), axis=1, keepdims=True
    ) - 1.0
    pick = ones_where(row_of_slot == iota((fslots, rows), 1))
    load_modes.wait()
    pair = NZ * FCAP
    line = nplane * FCAP
    in_plane = pl.ds(pl.multiple_of(plane * pair, pair), pair)
    in_line = pl.ds(pl.multiple_of(zpos * line, line), line)
    order = [e * quarter + jj for jj in range(quarter) for e in range(2)]

    def gather(j):
        got = dot(pick, whole[own_blocks, :, j * LANES : (j + 2) * LANES].reshape(rows, 2 * LANES))
        for i in range(2):
            over_plane[j + i] = got[:, i * LANES : (i + 1) * LANES].astype(bf16)
            plane_recv[j + i, in_plane, :] = over_plane[j + i, in_plane, :]

    def send_over_plane(j):
        def send(k, carry):
            dest = lax.rem(plane + k, nplane)
            pltpu.make_async_remote_copy(
                over_plane.at[j, pl.ds(pl.multiple_of(dest * pair, pair), pair)],
                plane_recv.at[j, in_plane],
                plane_sem, plane_recv_sem.at[j], **to(dest * NZ + zpos, half),
            ).start()
            return carry

        lax.fori_loop(1, nplane, send, 0, unroll=5)

    gather(0)
    gather(quarter)

    pl.semaphore_wait(barrier, NZ - 1 + 2 * nplane - 1)
    modes_copy = pltpu.make_async_remote_copy(
        whole.at[own_blocks], whole.at[own_blocks], modes_sem.at[0], modes_sem.at[1], **to(comp, other)
    )
    modes_copy.start()
    for j in order[:4]:
        send_over_plane(j)
    gather(2)
    gather(quarter + 2)
    for j in order[4:]:
        send_over_plane(j)

    turn = lax.broadcasted_iota(jnp.int32, (fslots, fslots), 0)
    turned = ((turn // FCAP) & (nplane - 1)) * pair + turn // line * FCAP + (turn & (FCAP - 1))
    regroup[...] = ones_where(turned == lax.broadcasted_iota(jnp.int32, (fslots, fslots), 1))

    def plane_wait(j):
        landed = plane_recv.at[j, pl.ds(0, (nplane - 1) * pair)]
        return pltpu.make_async_remote_copy(
            landed, landed, plane_sem, plane_recv_sem.at[j], **to(comp, other)
        )

    def z_wait(j):
        landed = z_recv.at[j, pl.ds(0, (NZ - 1) * line)]
        return pltpu.make_async_remote_copy(
            landed, landed, z_sem, z_recv_sem.at[j], **to(comp, other)
        )

    def pass_on(j):
        plane_wait(j).wait_recv()
        over_z[j] = dot(regroup[...], plane_recv[j]).astype(bf16)
        z_recv[j, in_line, :] = over_z[j, in_line, :]

        def send(k, carry):
            dest = lax.rem(zpos + k, NZ)
            pltpu.make_async_remote_copy(
                over_z.at[j, pl.ds(pl.multiple_of(dest * line, line), line)],
                z_recv.at[j, in_line],
                z_sem, z_recv_sem.at[j], **to(plane * NZ + dest, half),
            ).start()
            return carry

        lax.fori_loop(1, NZ, send, 0, unroll=7)

    for load in loads[4:7]:
        load.wait()
    owner = joint_owner[...].astype(f32)
    local = joint_local[...].astype(f32)
    njoint = owner.shape[1]
    square = (njoint, njoint)
    before = (as_column(owner) == owner) & (iota(square, 0) < iota(square, 1))
    position = jnp.sum(jnp.where(before, 1.0, 0.0), axis=0, keepdims=True)
    group = NZ * JCAP
    unit = group // 2
    owner_z = joint_owner[...] & (NZ - 1)
    owner_plane = joint_owner[...] // NZ
    slot_in_unit = (owner_z // 2) * JCAP + position.astype(jnp.int32)
    jslot = (owner_plane * group + (owner_z & 1) * unit + slot_in_unit).astype(f32)
    lane = slot_in_unit + (plane & 7) * unit
    of_plane = ones_where(
        lax.broadcasted_iota(jnp.int32, (2 * nplane, njoint), 0) == owner_plane * 2 + (owner_z & 1)
    )
    at_lane = jnp.where(
        lax.broadcasted_iota(jnp.int32, (LANES, njoint), 0) == lane, local + 1.0, 0.0
    ).astype(bf16)
    ids = lax.dot_general(of_plane, at_lane, (((1,), (1,)), ((), ())), preferred_element_type=f32)
    for d in range(2 * nplane):
        id_send[d] = ids[d : d + 1, :]
    id_recv[pl.ds(2 * here, 2)] = id_send[pl.ds(2 * plane, 2)]

    def id_copy(k, b):
        dest = lax.rem(plane + k, nplane)
        return pltpu.make_async_remote_copy(
            id_send.at[pl.ds(2 * dest, 2)], id_recv.at[pl.ds(2 * here, 2)],
            id_sem.at[0], id_sem.at[1], **to(dest * NZ + zpos, b),
        )

    def send_ids(k, carry):
        id_copy(k, half).start()
        id_copy(k, other).start()
        return carry

    id_copy(0, other).start()
    lax.fori_loop(1, nplane, send_ids, 0, unroll=5)

    pass_on(order[0])

    at_row = iota((rows, LANES), 0) == frow
    slot_of_row = jnp.sum(jnp.where(at_row, in_slot + 1.0, 0.0), axis=1, keepdims=True) - 1.0
    bolt[...] = jnp.broadcast_to(
        jnp.sum(jnp.where(at_row, fstiff, 0.0), axis=1, keepdims=True), bolt.shape
    )
    select_row[...] = ones_where(slot_of_row == iota((rows, fslots), 1))
    by_row = as_column(frow) == iota((LANES, rows), 1)
    slots_along = jnp.sum(jnp.where(by_row, as_column(in_slot) + 1.0, 0.0), axis=0, keepdims=True)
    bolts_along = jnp.sum(jnp.where(by_row, as_column(fstiff), 0.0), axis=0, keepdims=True)
    joint_row = jnp.sum(
        jnp.where(iota((jslots, njoint), 0) == jslot, joint_rows[...].astype(f32) + 1.0, 0.0),
        axis=1, keepdims=True,
    ) - 1.0
    takes = joint_row == iota((jslots, rows), 1)
    joint_select[...] = ones_where(takes)
    joint_slot = jnp.sum(jnp.where(takes, slots_along, 0.0), axis=1, keepdims=True) - 1.0
    joint_flange[...] = ones_where(joint_slot == iota((jslots, fslots), 1))
    joint_bolt[...] = jnp.broadcast_to(
        jnp.sum(jnp.where(takes, bolts_along, 0.0), axis=1, keepdims=True), joint_bolt.shape
    )

    pass_on(order[1])
    pass_on(order[2])

    loads[7].wait()
    load_stiff.wait()
    modes_copy.wait()

    half_cols = cols // 2

    def block_row(p):
        def run(r, carry):
            at = pl.ds(pl.multiple_of(r * BLOCK, BLOCK), BLOCK)
            for e in range(2):
                span = slice(e * cols + p * half_cols, e * cols + (p + 1) * half_cols)
                two = slice(p * half_cols, (p + 1) * half_cols)
                taken = jnp.concatenate(
                    [whole[block_cols[0, k, r], :, span] for k in range(NEIGH)], axis=0
                )
                own = whole[half * nblocks + r, :, span].astype(f32)
                value = dot(stiff[at, :], taken) + bolt[at, 0:1] * own
                top = value.astype(bf16)
                base[e, at, two] = value
                high[e, at, two] = top
                low[e, at, two] = (value - top.astype(f32)).astype(bf16)
            return carry

        return run

    def base_rows(p):
        two = slice(p * half_cols, (p + 1) * half_cols)
        for e in range(2):
            joint_base[e, :, two] = dot(joint_select[...], high[e, :, two]) + dot(
                joint_select[...], low[e, :, two]
            )

    def rows_copy(k, e, jj, g):
        dest = lax.rem(plane + k, nplane)
        return pltpu.make_async_remote_copy(
            rows_send.at[e * quarter + jj, pl.ds(pl.multiple_of(dest * group + g * unit, unit), unit)],
            rows_recv.at[jj, g, pl.ds(pl.multiple_of(here * unit, unit), unit)],
            rows_send_sem, rows_recv_sem.at[2 * jj + g], **to(dest * NZ + zpos, jnp.int32(e)),
        )

    def send_rows(e, jj, g):
        def send(k, carry):
            rows_copy(k, e, jj, g).start()
            return carry

        lax.fori_loop(1, nplane, send, 0, unroll=5)

        @pl.when(half != e)
        def _():
            rows_copy(0, e, jj, g).start()

        @pl.when(half == e)
        def _():
            rows_recv[jj, g, pl.ds(pl.multiple_of(here * unit, unit), unit), :] = rows_send[
                e * quarter + jj, pl.ds(pl.multiple_of(plane * group + g * unit, unit), unit), :
            ]

    def joint_rows_out(jj):
        span = slice(jj * LANES, (jj + 1) * LANES)
        for e in range(2):
            j = e * quarter + jj
            z_wait(j).wait_recv()
            part = z_recv[j]
            incoming[e, :, span] = part
            rows_send[j] = (
                joint_base[e, :, span] - joint_bolt[...] * dot(joint_flange[...], part)
            ).astype(bf16)
            send_rows(e, jj, 0)
        for e in range(2):
            send_rows(e, jj, 1)

    lax.fori_loop(0, nblocks // 2, block_row(0), 0)
    pass_on(order[3])
    lax.fori_loop(nblocks // 2, nblocks, block_row(0), 0)
    pass_on(order[4])
    pass_on(order[5])
    base_rows(0)
    joint_rows_out(0)
    pass_on(order[6])
    pass_on(order[7])
    joint_rows_out(1)
    lax.fori_loop(0, nblocks, block_row(1), 0)
    base_rows(1)
    joint_rows_out(2)
    joint_rows_out(3)

    id_all = id_recv.at[pl.ds(0, 2 * (2 * nplane - 1))]
    id_wait = pltpu.make_async_remote_copy(
        id_all, id_all, id_sem.at[0], id_sem.at[1], **to(comp, other)
    )
    id_wait.wait_recv()
    lane_z = ((lax.broadcasted_iota(jnp.int32, (1, LANES), 1) & (unit - 1)) // JCAP).astype(f32)
    sources = LANES // unit
    for g in range(2):
        for b in range(2 * nplane // sources):
            one = id_recv[2 * sources * b + g]
            for i in range(1, sources):
                one = one + id_recv[2 * (sources * b + i) + g]
            key = jnp.where(one > 0.5, lane_z * JOWN + one - 1.0, -1.0)
            place[g, :, b * LANES : (b + 1) * LANES] = ones_where(
                iota((NZ // 2 * JOWN, LANES), 0) == key
            )

    step = 256

    def round_rows(which, m):
        at = pl.ds(pl.multiple_of(m * step, step), step)
        partner = dot(select_row[at, :], incoming[which])
        return (base[which, at, :] - bolt[at, 0:1] * partner).astype(bf16)

    def round_other(m, carry):
        round_send[pl.ds(pl.multiple_of(m * step, step), step), :] = round_rows(other, m)
        return carry

    def round_own(m, carry):
        at = pl.ds(pl.multiple_of(half * rows + m * step, step), step)
        round_full[at, :] = round_rows(half, m)
        return carry

    lax.fori_loop(0, rows // step, round_other, 0)
    round_copy = pltpu.make_async_remote_copy(
        round_send, round_full.at[own_rows], round_sem.at[0], round_sem.at[1], **to(comp, other)
    )
    round_copy.start()

    factor = 1.0 / math.sqrt(2 * rows)
    got_rows = pl.ds(0, (2 * nplane - 1) * unit)
    width = iface // quarter

    def add_up(jj, g):
        landed = rows_recv.at[jj, g, got_rows]
        pltpu.make_async_remote_copy(
            landed, landed, rows_send_sem, rows_recv_sem.at[2 * jj + g], **to(comp, other)
        ).wait_recv()
        part_send[jj, g] = dot(place[g], rows_recv[jj, g]).astype(bf16)
        mine = pl.ds(pl.multiple_of(zpos * JOWN, JOWN), JOWN)
        for q in range(NZ // 2):
            dest = 2 * q + g
            rows_there = pl.ds(q * JOWN, JOWN)

            @pl.when(dest != zpos)
            def _():
                pltpu.make_async_remote_copy(
                    part_send.at[jj, g, rows_there],
                    part_recv.at[jj, mine],
                    part_send_sem, part_recv_sem.at[jj], **to(plane * NZ + dest, half),
                ).start()

            @pl.when(dest == zpos)
            def _():
                part_recv[jj, mine, :] = part_send[jj, g, rows_there, :]

    def project(piece):
        span = slice(piece * width, (piece + 1) * width)
        reduced[0, span, :] = (
            lax.dot_general(
                whole[:, :, span].reshape(2 * rows, width), round_full[...], (((0,), (0,)), ((), ())),
                preferred_element_type=f32,
            )
            * factor
        )

    add_up(0, 0)
    add_up(0, 1)
    lax.fori_loop(0, rows // step, round_own, 0)
    add_up(1, 0)
    add_up(1, 1)
    round_copy.wait()
    project(0)
    project(1)
    add_up(2, 0)
    add_up(2, 1)
    project(2)
    add_up(3, 0)
    add_up(3, 1)
    project(3)

    for jj in range(quarter):
        landed = part_recv.at[jj, pl.ds(0, (NZ - 1) * JOWN)]
        pltpu.make_async_remote_copy(
            landed, landed, part_send_sem, part_recv_sem.at[jj], **to(comp, other)
        ).wait_recv()
        total = part_recv[jj, 0:JOWN, :].astype(f32)
        for z in range(1, NZ):
            total = total + part_recv[jj, z * JOWN : (z + 1) * JOWN, :].astype(f32)
        forces[:, jj * LANES : (jj + 1) * LANES] = total

    for j in order:
        plane_wait(j).wait_send()
        z_wait(j).wait_send()
    id_wait.wait_send()

    for jj in range(quarter):
        for g in range(2):
            gone = rows_recv.at[jj, g, got_rows]
            pltpu.make_async_remote_copy(
                gone, gone, rows_send_sem, rows_recv_sem.at[2 * jj + g], **to(comp, other)
            ).wait_send()
        gone = part_recv.at[jj, pl.ds(0, (NZ - 1) * JOWN)]
        pltpu.make_async_remote_copy(
            gone, gone, part_send_sem, part_recv_sem.at[jj], **to(comp, other)
        ).wait_send()


def body(*args):
    modes, stiff = args[0], args[1]
    ncomp = lax.axis_size("comp")
    rows, iface = modes.shape[1:]
    cols = iface // 2
    quarter = cols // LANES
    chunks = 2 * quarter
    width = stiff.shape[2]
    fslots, jslots = ncomp * FCAP, ncomp * JCAP
    nplane = ncomp // NZ
    dma = pltpu.SemaphoreType.DMA
    vmem = pl.BlockSpec(memory_space=pltpu.VMEM)
    hbm = pl.BlockSpec(memory_space=pl.ANY)
    scratch = [pltpu.SMEM((1, NEIGH, rows // BLOCK), jnp.int32)]
    scratch += [pltpu.VMEM(a.shape, a.dtype) for a in args[3:]]
    scratch += [
        pltpu.VMEM((2 * rows // BLOCK, BLOCK, iface), bf16),
        pltpu.VMEM((rows, width), bf16),
        pltpu.VMEM((8, LANES), f32),
        pltpu.VMEM((chunks, fslots, LANES), bf16),
        pltpu.VMEM((chunks, fslots, LANES), bf16),
        pltpu.VMEM((fslots, fslots), bf16),
        pltpu.VMEM((chunks, fslots, LANES), bf16),
        pltpu.VMEM((chunks, fslots, LANES), bf16),
        pltpu.VMEM((2, fslots, cols), bf16),
        pltpu.VMEM((2, rows, cols), f32),
        pltpu.VMEM((2, rows, cols), bf16),
        pltpu.VMEM((2, rows, cols), bf16),
        pltpu.VMEM((rows, LANES), f32),
        pltpu.VMEM((rows, fslots), bf16),
        pltpu.VMEM((jslots, rows), bf16),
        pltpu.VMEM((jslots, fslots), bf16),
        pltpu.VMEM((jslots, LANES), f32),
        pltpu.VMEM((2, jslots, cols), f32),
        pltpu.VMEM((2 * nplane, 1, LANES), f32),
        pltpu.VMEM((4 * nplane, 1, LANES), f32),
        pltpu.VMEM((2, NZ // 2 * JOWN, jslots), bf16),
        pltpu.VMEM((2 * quarter, jslots, LANES), bf16),
        pltpu.VMEM((quarter, 2, jslots, LANES), bf16),
        pltpu.VMEM((rows, cols), bf16),
        pltpu.VMEM((2 * rows, cols), bf16),
        pltpu.VMEM((quarter, 2, NZ // 2 * JOWN, LANES), bf16),
        pltpu.VMEM((quarter, NZ * JOWN, LANES), bf16),
        dma((2,)), dma((8,)), dma, dma((chunks,)), dma, dma((chunks,)),
        dma((2,)), dma((2,)), dma, dma((chunks,)),
        dma((2,)), dma, dma((quarter,)),
    ]
    return pl.pallas_call(
        kernel,
        out_shape=(
            pltpu.VMEM((1, iface, cols), f32),
            pltpu.VMEM((JOWN, cols), f32),
        ),
        in_specs=[hbm] * 10,
        out_specs=(vmem, vmem),
        scratch_shapes=scratch,
        compiler_params=pltpu.CompilerParams(
            collective_id=0, has_side_effects=True, vmem_limit_bytes=56 << 20
        ),
    )(modes.reshape(rows // BLOCK, BLOCK, iface), stiff, jnp.swapaxes(args[2], 1, 2), *args[3:])


def solution(mesh):
    placed = (
        P("comp", "blk", None),
        P("comp", "blk", None),
        P("comp", "blk", None),
        P("comp", "blk"),
        P("comp", "blk"),
        P("comp", "blk"),
        P("comp", "blk"),
        P("comp", "blk"),
        P("comp", "blk"),
        P("comp", "blk"),
    )
    return jax.shard_map(
        body,
        mesh=mesh,
        in_specs=placed,
        out_specs=(P("comp", None, "blk"), P("comp", "blk")),
        check_vma=False,
    )
```

```python
import math

import jax
import jax.numpy as jnp
from jax import lax
from jax.experimental import pallas as pl
from jax.experimental.pallas import tpu as pltpu
from jax.sharding import PartitionSpec as P

MESH = pl.DeviceIdType.MESH
BLOCK = 64
NEIGH = 8
FCAP = 2
JCAP = 4
JOWN = 64
NZ = 8
LANES = 128
f32 = jnp.float32
bf16 = jnp.bfloat16


def iota(shape, dim):
    return lax.broadcasted_iota(jnp.int32, shape, dim).astype(f32)


def ones_where(mask):
    return jnp.where(mask, 1.0, 0.0).astype(bf16)


def dot(left, right):
    return jnp.dot(left, right, preferred_element_type=f32)


def as_column(row):
    n = row.shape[1]
    return jnp.sum(jnp.where(iota((n, n), 0) == iota((n, n), 1), row, 0.0), axis=1, keepdims=True)


def kernel(
    modes_hbm, stiff_hbm, block_cols_hbm, flange_rows_hbm, flange_dest_hbm, flange_match_hbm,
    flange_stiff_hbm, joint_rows_hbm, joint_owner_hbm, joint_local_hbm,
    reduced, forces,
    block_cols, flange_rows, flange_dest, flange_match, flange_stiff,
    joint_rows, joint_owner, joint_local,
    whole_0, whole_1, whole_2, whole_3, stiff, vec, over_plane, plane_recv, regroup, ungroup, over_z, z_recv, incoming, base, high, low,
    bolt, select_row, joint_select, joint_flange, joint_bolt, joint_place, joint_base,
    id_send, id_recv, place, rows_send, rows_recv, round_send, round_full,
    part_send, part_recv,
    load_sem, small_sem, plane_sem, plane_recv_sem, z_sem, z_recv_sem, modes_sem, id_sem, rows_send_sem, rows_recv_sem,
    round_sem, part_send_sem, part_recv_sem,
):
    ncomp = lax.axis_size("comp")
    nplane = ncomp // NZ
    comp = lax.axis_index("comp")
    half = lax.axis_index("blk")
    other = 1 - half
    plane = comp // NZ
    zpos = lax.rem(comp, NZ)
    whole = (whole_0, whole_1, whole_2, whole_3)
    rows, cols = stiff.shape[0], forces.shape[1]
    iface = 2 * cols
    nflange = flange_rows.shape[1]
    fslots = ncomp * FCAP
    jslots = ncomp * JCAP
    chunks = iface // LANES
    quarter = chunks // 2
    own_rows = pl.ds(pl.multiple_of(half * rows, rows), rows)
    nblocks = rows // BLOCK
    own_blocks = pl.ds(half * nblocks, nblocks)
    here = half * nplane + plane

    def to(c, b):
        return dict(device_id={"comp": c, "blk": b}, device_id_type=MESH)

    load_modes = [
        [
            pltpu.make_async_copy(
                modes_hbm.at[:, :, pl.ds(e * cols + q * LANES, LANES)],
                whole[q].at[own_blocks, :, pl.ds(e * LANES, LANES)],
                load_sem.at[2 * q + e],
            )
            for e in range(2)
        ]
        for q in range(quarter)
    ]
    load_stiff = pltpu.make_async_copy(stiff_hbm.at[0], stiff, load_sem.at[chunks])
    loads = [
        pltpu.make_async_copy(source, target, small_sem.at[i])
        for i, (source, target) in enumerate(
            (
                (flange_rows_hbm, flange_rows),
                (flange_dest_hbm, flange_dest),
                (flange_match_hbm, flange_match),
                (flange_stiff_hbm, flange_stiff),
                (joint_rows_hbm, joint_rows),
                (joint_owner_hbm, joint_owner),
                (joint_local_hbm, joint_local),
                (block_cols_hbm, block_cols),
            )
        )
    ]
    for load in loads[:4]:
        load.start()
    for q in range(quarter):
        for load in load_modes[q]:
            load.start()
    for load in loads[4:]:
        load.start()
    load_stiff.start()

    barrier = pltpu.get_barrier_semaphore()

    def greet_z(k, carry):
        pl.semaphore_signal(barrier, inc=1, **to(plane * NZ + lax.rem(zpos + k, NZ), half))
        return carry

    def greet_plane(k, carry):
        there = lax.rem(plane + k, nplane) * NZ + zpos
        pl.semaphore_signal(barrier, inc=1, **to(there, other))
        pl.semaphore_signal(barrier, inc=1, **to(there, half))
        return carry

    lax.fori_loop(1, NZ, greet_z, 0, unroll=7)
    lax.fori_loop(1, nplane, greet_plane, 0, unroll=5)
    pl.semaphore_signal(barrier, inc=1, **to(comp, other))

    for load in loads[:4]:
        load.wait()
    vec[...] = jnp.full(vec.shape, -1.0, f32)
    parity = lax.broadcasted_iota(jnp.int32, (1, nflange), 1) & 1
    vec[0:1, 0:nflange] = flange_rows[...].astype(f32)
    vec[1:2, 0:nflange] = (flange_dest[...] * FCAP + parity).astype(f32)
    vec[2:3, 0:nflange] = (
        ((flange_dest[...] & (NZ - 1)) * nplane + flange_dest[...] // NZ) * FCAP
        + (flange_match[...] & 1)
    ).astype(f32)
    vec[3:4, 0:nflange] = flange_stiff[...]
    frow, out_slot, in_slot, fstiff = vec[0:1, :], vec[1:2, :], vec[2:3, :], vec[3:4, :]
    row_of_slot = jnp.sum(
        jnp.where(iota((fslots, LANES), 0) == out_slot, frow + 1.0, 0.0), axis=1, keepdims=True
    ) - 1.0
    pick = ones_where(row_of_slot == iota((fslots, rows), 1))
    last = quarter - 1
    pair = NZ * FCAP
    line = nplane * FCAP
    in_plane = pl.ds(pl.multiple_of(plane * pair, pair), pair)
    in_line = pl.ds(pl.multiple_of(zpos * line, line), line)

    turn = lax.broadcasted_iota(jnp.int32, (fslots, fslots), 0)
    turned = ((turn // FCAP) & (nplane - 1)) * pair + turn // line * FCAP + (turn & (FCAP - 1))
    regroup[...] = ones_where(turned == lax.broadcasted_iota(jnp.int32, (fslots, fslots), 1))
    back = ((turn // FCAP) & (NZ - 1)) * line + turn // pair * FCAP + (turn & (FCAP - 1))
    ungroup[...] = ones_where(back == lax.broadcasted_iota(jnp.int32, (fslots, fslots), 1))

    def gather(q):
        for load in load_modes[q]:
            load.wait()
        got = dot(pick, whole[q][own_blocks].reshape(rows, 2 * LANES))
        for e in range(2):
            j = e * quarter + q
            over_plane[j] = got[:, e * LANES : (e + 1) * LANES].astype(bf16)
            if q < last:
                plane_recv[j, in_plane, :] = over_plane[j, in_plane, :]

    def send_over_plane(j):
        def send(k, carry):
            dest = lax.rem(plane + k, nplane)
            pltpu.make_async_remote_copy(
                over_plane.at[j, pl.ds(pl.multiple_of(dest * pair, pair), pair)],
                plane_recv.at[j, in_plane],
                plane_sem, plane_recv_sem.at[j], **to(dest * NZ + zpos, half),
            ).start()
            return carry

        lax.fori_loop(1, nplane, send, 0, unroll=5)

    gather(0)

    pl.semaphore_wait(barrier, NZ - 1 + 2 * nplane - 1)
    modes_copies = [
        pltpu.make_async_remote_copy(
            whole[q].at[own_blocks], whole[q].at[own_blocks], modes_sem.at[0, q], modes_sem.at[1, q],
            **to(comp, other),
        )
        for q in range(quarter)
    ]
    def send_all():
        for e in range(2):
            send_over_plane(e * quarter)
        gather(last)
        for e in range(2):
            j = e * quarter + last
            over_z[j] = dot(regroup[...], over_plane[j]).astype(bf16)
            send_over_z(j)
        modes_copies[0].start()
        for q in range(1, last):
            gather(q)
            for e in range(2):
                send_over_plane(e * quarter + q)
            modes_copies[q].start()
        modes_copies[last].start()

    def plane_wait(j):
        landed = plane_recv.at[j, pl.ds(0, (nplane - 1) * pair)]
        return pltpu.make_async_remote_copy(
            landed, landed, plane_sem, plane_recv_sem.at[j], **to(comp, other)
        )

    def z_wait(j):
        landed = z_recv.at[j, pl.ds(0, (NZ - 1) * line)]
        return pltpu.make_async_remote_copy(
            landed, landed, z_sem, z_recv_sem.at[j], **to(comp, other)
        )

    def pass_on(q):
        for e in range(2):
            pass_chunk(e * quarter + q)

    def send_over_z(j):
        z_recv[j, in_line, :] = over_z[j, in_line, :]

        def send(k, carry):
            dest = lax.rem(zpos + k, NZ)
            pltpu.make_async_remote_copy(
                over_z.at[j, pl.ds(pl.multiple_of(dest * line, line), line)],
                z_recv.at[j, in_line],
                z_sem, z_recv_sem.at[j], **to(plane * NZ + dest, half),
            ).start()
            return carry

        lax.fori_loop(1, NZ, send, 0, unroll=7)

    def pass_chunk(j):
        if j % quarter < last:
            plane_wait(j).wait_recv()
            over_z[j] = dot(regroup[...], plane_recv[j]).astype(bf16)
            send_over_z(j)
        else:
            z_wait(j).wait_recv()
            over_plane[j] = dot(ungroup[...], z_recv[j]).astype(bf16)
            plane_recv[j, in_plane, :] = over_plane[j, in_plane, :]
            send_over_plane(j)

    send_all()

    pass_on(0)

    for load in loads[4:7]:
        load.wait()
    owner = joint_owner[...].astype(f32)
    local = joint_local[...].astype(f32)
    njoint = owner.shape[1]
    square = (njoint, njoint)
    before = (as_column(owner) == owner) & (iota(square, 0) < iota(square, 1))
    position = jnp.sum(jnp.where(before, 1.0, 0.0), axis=0, keepdims=True)
    group = NZ * JCAP
    unit = group // 2
    owner_z = joint_owner[...] & (NZ - 1)
    owner_plane = joint_owner[...] // NZ
    slot_in_unit = (owner_z // 2) * JCAP + position.astype(jnp.int32)
    jslot = (owner_plane * group + (owner_z & 1) * unit + slot_in_unit).astype(f32)
    lane = slot_in_unit + (plane & 7) * unit
    of_plane = ones_where(
        lax.broadcasted_iota(jnp.int32, (2 * nplane, njoint), 0) == owner_plane * 2 + (owner_z & 1)
    )
    at_lane = jnp.where(
        lax.broadcasted_iota(jnp.int32, (LANES, njoint), 0) == lane, local + 1.0, 0.0
    ).astype(bf16)
    ids = lax.dot_general(of_plane, at_lane, (((1,), (1,)), ((), ())), preferred_element_type=f32)
    for d in range(2 * nplane):
        id_send[d] = ids[d : d + 1, :]
    id_recv[pl.ds(2 * here, 2)] = id_send[pl.ds(2 * plane, 2)]

    def id_copy(k, b):
        dest = lax.rem(plane + k, nplane)
        return pltpu.make_async_remote_copy(
            id_send.at[pl.ds(2 * dest, 2)], id_recv.at[pl.ds(2 * here, 2)],
            id_sem.at[0], id_sem.at[1], **to(dest * NZ + zpos, b),
        )

    def send_ids(k, carry):
        id_copy(k, half).start()
        id_copy(k, other).start()
        return carry

    id_copy(0, other).start()
    lax.fori_loop(1, nplane, send_ids, 0, unroll=5)

    at_row = iota((rows, LANES), 0) == frow
    slot_of_row = jnp.sum(jnp.where(at_row, in_slot + 1.0, 0.0), axis=1, keepdims=True) - 1.0
    bolt[...] = jnp.broadcast_to(
        jnp.sum(jnp.where(at_row, fstiff, 0.0), axis=1, keepdims=True), bolt.shape
    )
    select_row[...] = ones_where(slot_of_row == iota((rows, fslots), 1))
    by_row = as_column(frow) == iota((LANES, rows), 1)
    slots_along = jnp.sum(jnp.where(by_row, as_column(in_slot) + 1.0, 0.0), axis=0, keepdims=True)
    bolts_along = jnp.sum(jnp.where(by_row, as_column(fstiff), 0.0), axis=0, keepdims=True)
    takes = as_column(joint_rows[...].astype(f32)) == iota((njoint, rows), 1)
    joint_select[...] = ones_where(takes)
    joint_slot = jnp.sum(jnp.where(takes, slots_along, 0.0), axis=1, keepdims=True) - 1.0
    joint_flange[...] = ones_where(joint_slot == iota((njoint, fslots), 1))
    joint_bolt[...] = jnp.broadcast_to(
        jnp.sum(jnp.where(takes, bolts_along, 0.0), axis=1, keepdims=True), joint_bolt.shape
    )
    joint_place[...] = ones_where(iota((jslots, njoint), 0) == jslot)

    loads[7].wait()
    load_stiff.wait()


    def block_row(q):
        def run(r, carry):
            at = pl.ds(pl.multiple_of(r * BLOCK, BLOCK), BLOCK)
            taken = jnp.concatenate([whole[q][block_cols[0, k, r]] for k in range(NEIGH)], axis=0)
            own = whole[q][half * nblocks + r].astype(f32)
            value = dot(stiff[at, :], taken)
            for e in range(2):
                span = slice(e * LANES, (e + 1) * LANES)
                here_value = value[:, span] + bolt[at, :] * own[:, span]
                top = here_value.astype(bf16)
                base[e, q, at, :] = here_value
                high[e, q, at, :] = top
                low[e, q, at, :] = (here_value - top.astype(f32)).astype(bf16)
            return carry

        return run

    def product(q):
        modes_copies[q].wait()
        lax.fori_loop(0, nblocks, block_row(q), 0, unroll=16)
        sides = [jnp.concatenate([part[0, q], part[1, q]], axis=1) for part in (high, low)]
        joint_base[q] = dot(joint_select[...], sides[0]) + dot(joint_select[...], sides[1])

    def rows_copy(k, e, jj, g):
        dest = lax.rem(plane + k, nplane)
        return pltpu.make_async_remote_copy(
            rows_send.at[e * quarter + jj, pl.ds(pl.multiple_of(dest * group + g * unit, unit), unit)],
            rows_recv.at[jj, g, pl.ds(pl.multiple_of(here * unit, unit), unit)],
            rows_send_sem, rows_recv_sem.at[2 * jj + g], **to(dest * NZ + zpos, jnp.int32(e)),
        )

    def send_rows(e, jj, g):
        def send(k, carry):
            rows_copy(k, e, jj, g).start()
            return carry

        lax.fori_loop(1, nplane, send, 0, unroll=5)

        @pl.when(half != e)
        def _():
            rows_copy(0, e, jj, g).start()

        @pl.when(half == e)
        def _():
            rows_recv[jj, g, pl.ds(pl.multiple_of(here * unit, unit), unit), :] = rows_send[
                e * quarter + jj, pl.ds(pl.multiple_of(plane * group + g * unit, unit), unit), :
            ]

    def joint_rows_out(jj):
        span = slice(jj * LANES, (jj + 1) * LANES)
        for e in range(2):
            j = e * quarter + jj
            if jj < last:
                z_wait(j).wait_recv()
                part = z_recv[j]
            else:
                plane_wait(j).wait_recv()
                part = dot(regroup[...], plane_recv[j]).astype(bf16)
            incoming[e, :, span] = part
            entries = (
                joint_base[jj, :, e * LANES : (e + 1) * LANES]
                - joint_bolt[...] * dot(joint_flange[...], part)
            ).astype(bf16)
            rows_send[j] = dot(joint_place[...], entries).astype(bf16)
            send_rows(e, jj, 0)
        for e in range(2):
            send_rows(e, jj, 1)

    product(0)
    pass_on(1)
    joint_rows_out(0)
    pass_on(2)
    pass_on(3)
    product(1)
    joint_rows_out(1)
    product(2)
    joint_rows_out(2)

    id_all = id_recv.at[pl.ds(0, 2 * (2 * nplane - 1))]
    id_wait = pltpu.make_async_remote_copy(
        id_all, id_all, id_sem.at[0], id_sem.at[1], **to(comp, other)
    )
    id_wait.wait_recv()
    lane_z = ((lax.broadcasted_iota(jnp.int32, (1, LANES), 1) & (unit - 1)) // JCAP).astype(f32)
    sources = LANES // unit
    for g in range(2):
        for b in range(2 * nplane // sources):
            one = id_recv[2 * sources * b + g]
            for i in range(1, sources):
                one = one + id_recv[2 * (sources * b + i) + g]
            key = jnp.where(one > 0.5, lane_z * JOWN + one - 1.0, -1.0)
            place[g, :, b * LANES : (b + 1) * LANES] = ones_where(
                iota((NZ // 2 * JOWN, LANES), 0) == key
            )

    factor = 1.0 / math.sqrt(2 * rows)
    got_rows = pl.ds(0, (2 * nplane - 1) * unit)

    def add_up(jj, g):
        landed = rows_recv.at[jj, g, got_rows]
        pltpu.make_async_remote_copy(
            landed, landed, rows_send_sem, rows_recv_sem.at[2 * jj + g], **to(comp, other)
        ).wait_recv()
        part_send[jj, g] = dot(place[g], rows_recv[jj, g]).astype(bf16)
        mine = pl.ds(pl.multiple_of(zpos * JOWN, JOWN), JOWN)
        for q in range(NZ // 2):
            dest = 2 * q + g
            rows_there = pl.ds(q * JOWN, JOWN)

            @pl.when(dest != zpos)
            def _():
                pltpu.make_async_remote_copy(
                    part_send.at[jj, g, rows_there],
                    part_recv.at[jj, mine],
                    part_send_sem, part_recv_sem.at[jj], **to(plane * NZ + dest, half),
                ).start()

            @pl.when(dest == zpos)
            def _():
                part_recv[jj, mine, :] = part_send[jj, g, rows_there, :]

    def project(q):
        full = lax.dot_general(
            whole[q][...].reshape(2 * rows, 2 * LANES), round_full[...], (((0,), (0,)), ((), ())),
            preferred_element_type=f32,
        )
        for e in range(2):
            reduced[0, e * cols + q * LANES : e * cols + (q + 1) * LANES, :] = (
                full[e * LANES : (e + 1) * LANES] * factor
            )

    step = 256

    def round_rows(which, m, target, first):
        at = pl.ds(pl.multiple_of(m * step, step), step)
        partner = dot(select_row[at, :], incoming[which])
        for q in range(quarter):
            span = slice(q * LANES, (q + 1) * LANES)
            target[pl.ds(pl.multiple_of(first + m * step, step), step), span] = (
                base[which, q, at, :] - bolt[at, :] * partner[:, span]
            ).astype(bf16)

    def round_other(m, carry):
        round_rows(other, m, round_send, 0)
        return carry

    def round_own(m, carry):
        round_rows(half, m, round_full, half * rows)
        return carry

    round_copy = pltpu.make_async_remote_copy(
        round_send, round_full.at[own_rows], round_sem.at[0], round_sem.at[1], **to(comp, other)
    )

    add_up(0, 0)
    product(3)
    joint_rows_out(3)
    add_up(0, 1)
    add_up(1, 0)
    add_up(1, 1)
    lax.fori_loop(0, rows // step, round_other, 0)
    round_copy.start()
    add_up(2, 0)
    lax.fori_loop(0, rows // step, round_own, 0)
    add_up(2, 1)
    round_copy.wait()
    project(0)
    add_up(3, 0)
    project(1)
    add_up(3, 1)
    project(2)
    project(3)

    for jj in range(quarter):
        landed = part_recv.at[jj, pl.ds(0, (NZ - 1) * JOWN)]
        pltpu.make_async_remote_copy(
            landed, landed, part_send_sem, part_recv_sem.at[jj], **to(comp, other)
        ).wait_recv()
        total = part_recv[jj, 0:JOWN, :].astype(f32)
        for z in range(1, NZ):
            total = total + part_recv[jj, z * JOWN : (z + 1) * JOWN, :].astype(f32)
        forces[:, jj * LANES : (jj + 1) * LANES] = total

    for j in range(chunks):
        plane_wait(j).wait_send()
        z_wait(j).wait_send()
    id_wait.wait_send()

    for jj in range(quarter):
        for g in range(2):
            gone = rows_recv.at[jj, g, got_rows]
            pltpu.make_async_remote_copy(
                gone, gone, rows_send_sem, rows_recv_sem.at[2 * jj + g], **to(comp, other)
            ).wait_send()
        gone = part_recv.at[jj, pl.ds(0, (NZ - 1) * JOWN)]
        pltpu.make_async_remote_copy(
            gone, gone, part_send_sem, part_recv_sem.at[jj], **to(comp, other)
        ).wait_send()


def store(reduced, forces, reduced_hbm, forces_hbm, sem):
    copies = [
        pltpu.make_async_copy(reduced, reduced_hbm, sem.at[0]),
        pltpu.make_async_copy(forces, forces_hbm, sem.at[1]),
    ]
    for copy in copies:
        copy.start()
    for copy in copies:
        copy.wait()


def body(*args):
    modes, stiff = args[0], args[1]
    ncomp = lax.axis_size("comp")
    rows, iface = modes.shape[1:]
    cols = iface // 2
    quarter = cols // LANES
    chunks = 2 * quarter
    width, njoint = stiff.shape[2], args[7].shape[1]
    fslots, jslots = ncomp * FCAP, ncomp * JCAP
    nplane = ncomp // NZ
    dma = pltpu.SemaphoreType.DMA
    vmem = pl.BlockSpec(memory_space=pltpu.VMEM)
    hbm = pl.BlockSpec(memory_space=pl.ANY)
    scratch = [pltpu.SMEM((1, NEIGH, rows // BLOCK), jnp.int32)]
    scratch += [pltpu.VMEM(a.shape, a.dtype) for a in args[3:]]
    scratch += [pltpu.VMEM((2 * rows // BLOCK, BLOCK, 2 * LANES), bf16)] * quarter
    scratch += [
        pltpu.VMEM((rows, width), bf16),
        pltpu.VMEM((8, LANES), f32),
        pltpu.VMEM((chunks, fslots, LANES), bf16),
        pltpu.VMEM((chunks, fslots, LANES), bf16),
        pltpu.VMEM((fslots, fslots), bf16),
        pltpu.VMEM((fslots, fslots), bf16),
        pltpu.VMEM((chunks, fslots, LANES), bf16),
        pltpu.VMEM((chunks, fslots, LANES), bf16),
        pltpu.VMEM((2, fslots, cols), bf16),
        pltpu.VMEM((2, quarter, rows, LANES), f32),
        pltpu.VMEM((2, quarter, rows, LANES), bf16),
        pltpu.VMEM((2, quarter, rows, LANES), bf16),
        pltpu.VMEM((rows, LANES), f32),
        pltpu.VMEM((rows, fslots), bf16),
        pltpu.VMEM((njoint, rows), bf16),
        pltpu.VMEM((njoint, fslots), bf16),
        pltpu.VMEM((njoint, LANES), f32),
        pltpu.VMEM((jslots, njoint), bf16),
        pltpu.VMEM((quarter, njoint, 2 * LANES), f32),
        pltpu.VMEM((2 * nplane, 1, LANES), f32),
        pltpu.VMEM((4 * nplane, 1, LANES), f32),
        pltpu.VMEM((2, NZ // 2 * JOWN, jslots), bf16),
        pltpu.VMEM((2 * quarter, jslots, LANES), bf16),
        pltpu.VMEM((quarter, 2, jslots, LANES), bf16),
        pltpu.VMEM((rows, cols), bf16),
        pltpu.VMEM((2 * rows, cols), bf16),
        pltpu.VMEM((quarter, 2, NZ // 2 * JOWN, LANES), bf16),
        pltpu.VMEM((quarter, NZ * JOWN, LANES), bf16),
        dma((chunks + 1,)), dma((8,)), dma, dma((chunks,)), dma, dma((chunks,)),
        dma((2, quarter)), dma((2,)), dma, dma((chunks,)),
        dma((2,)), dma, dma((quarter,)),
    ]
    results = pl.pallas_call(
        kernel,
        out_shape=(
            pltpu.VMEM((1, iface, cols), f32),
            pltpu.VMEM((JOWN, cols), f32),
        ),
        in_specs=[hbm] * 10,
        out_specs=(vmem, vmem),
        scratch_shapes=scratch,
        compiler_params=pltpu.CompilerParams(
            collective_id=0, has_side_effects=True, vmem_limit_bytes=56 << 20
        ),
    )(modes.reshape(rows // BLOCK, BLOCK, iface), stiff, jnp.swapaxes(args[2], 1, 2), *args[3:])
    return pl.pallas_call(
        store,
        out_shape=tuple(jax.ShapeDtypeStruct(r.shape, r.dtype) for r in results),
        in_specs=[vmem, vmem],
        out_specs=(hbm, hbm),
        scratch_shapes=[dma((2,))],
    )(*(pltpu.with_memory_space_constraint(r, pltpu.VMEM) for r in results))


def solution(mesh):
    placed = (
        P("comp", "blk", None),
        P("comp", "blk", None),
        P("comp", "blk", None),
        P("comp", "blk"),
        P("comp", "blk"),
        P("comp", "blk"),
        P("comp", "blk"),
        P("comp", "blk"),
        P("comp", "blk"),
        P("comp", "blk"),
    )
    return jax.shard_map(
        body,
        mesh=mesh,
        in_specs=placed,
        out_specs=(P("comp", None, "blk"), P("comp", "blk")),
        check_vma=False,
    )
```

```python
import math

import jax
import jax.numpy as jnp
from jax import lax
from jax.experimental import pallas as pl
from jax.experimental.pallas import tpu as pltpu
from jax.sharding import PartitionSpec as P

MESH = pl.DeviceIdType.MESH
BLOCK = 64
NEIGH = 8
FCAP = 2
JCAP = 4
JOWN = 64
NZ = 8
LANES = 128
f32 = jnp.float32
bf16 = jnp.bfloat16


def iota(shape, dim):
    return lax.broadcasted_iota(jnp.int32, shape, dim).astype(f32)


def ones_where(mask):
    return jnp.where(mask, 1.0, 0.0).astype(bf16)


def dot(left, right):
    return jnp.dot(left, right, preferred_element_type=f32)


def as_column(row):
    n = row.shape[1]
    return jnp.sum(jnp.where(iota((n, n), 0) == iota((n, n), 1), row, 0.0), axis=1, keepdims=True)


def kernel(
    modes_hbm, stiff_hbm, block_cols_hbm, flange_rows_hbm, flange_dest_hbm, flange_match_hbm,
    flange_stiff_hbm, joint_rows_hbm, joint_owner_hbm, joint_local_hbm,
    reduced, forces,
    block_cols, flange_rows, flange_dest, flange_match, flange_stiff,
    joint_rows, joint_owner, joint_local,
    whole_0, whole_1, whole_2, whole_3, stiff, vec, over_plane, plane_recv, regroup, ungroup, over_z, z_recv, incoming, base, high, low,
    bolt, select_row, joint_select, joint_flange, joint_bolt, joint_place, joint_base,
    id_send, id_recv, place, rows_send, rows_recv, round_send, round_full,
    part_send, part_recv,
    load_sem, small_sem, plane_sem, plane_recv_sem, z_sem, z_recv_sem, modes_sem, id_sem, rows_send_sem, rows_recv_sem,
    round_sem, part_send_sem, part_recv_sem,
):
    ncomp = lax.axis_size("comp")
    nplane = ncomp // NZ
    comp = lax.axis_index("comp")
    half = lax.axis_index("blk")
    other = 1 - half
    plane = comp // NZ
    zpos = lax.rem(comp, NZ)
    whole = (whole_0, whole_1, whole_2, whole_3)
    rows, cols = stiff.shape[0], forces.shape[1]
    iface = 2 * cols
    nflange = flange_rows.shape[1]
    fslots = ncomp * FCAP
    jslots = ncomp * JCAP
    chunks = iface // LANES
    quarter = chunks // 2
    own_rows = pl.ds(pl.multiple_of(half * rows, rows), rows)
    nblocks = rows // BLOCK
    own_blocks = pl.ds(half * nblocks, nblocks)
    here = half * nplane + plane

    def to(c, b):
        return dict(device_id={"comp": c, "blk": b}, device_id_type=MESH)

    load_modes = [
        [
            pltpu.make_async_copy(
                modes_hbm.at[:, :, pl.ds(e * cols + q * LANES, LANES)],
                whole[q].at[own_blocks, :, pl.ds(e * LANES, LANES)],
                load_sem.at[2 * q + e],
            )
            for e in range(2)
        ]
        for q in range(quarter)
    ]
    load_stiff = pltpu.make_async_copy(stiff_hbm.at[0], stiff, load_sem.at[chunks])
    loads = [
        pltpu.make_async_copy(source, target, small_sem.at[i])
        for i, (source, target) in enumerate(
            (
                (flange_rows_hbm, flange_rows),
                (flange_dest_hbm, flange_dest),
                (flange_match_hbm, flange_match),
                (flange_stiff_hbm, flange_stiff),
                (joint_rows_hbm, joint_rows),
                (joint_owner_hbm, joint_owner),
                (joint_local_hbm, joint_local),
                (block_cols_hbm, block_cols),
            )
        )
    ]
    for load in loads[:4]:
        load.start()
    for q in range(quarter):
        for load in load_modes[q]:
            load.start()
    for load in loads[4:]:
        load.start()
    load_stiff.start()

    barrier = pltpu.get_barrier_semaphore()

    def greet_z(k, carry):
        pl.semaphore_signal(barrier, inc=1, **to(plane * NZ + lax.rem(zpos + k, NZ), half))
        return carry

    def greet_plane(k, carry):
        there = lax.rem(plane + k, nplane) * NZ + zpos
        pl.semaphore_signal(barrier, inc=1, **to(there, other))
        pl.semaphore_signal(barrier, inc=1, **to(there, half))
        return carry

    lax.fori_loop(1, NZ, greet_z, 0, unroll=7)
    lax.fori_loop(1, nplane, greet_plane, 0, unroll=15)
    pl.semaphore_signal(barrier, inc=1, **to(comp, other))

    for load in loads[:4]:
        load.wait()
    vec[...] = jnp.full(vec.shape, -1.0, f32)
    parity = lax.broadcasted_iota(jnp.int32, (1, nflange), 1) & 1
    vec[0:1, 0:nflange] = flange_rows[...].astype(f32)
    vec[1:2, 0:nflange] = (flange_dest[...] * FCAP + parity).astype(f32)
    vec[2:3, 0:nflange] = (
        ((flange_dest[...] & (NZ - 1)) * nplane + flange_dest[...] // NZ) * FCAP
        + (flange_match[...] & 1)
    ).astype(f32)
    vec[3:4, 0:nflange] = flange_stiff[...]
    frow, out_slot, in_slot, fstiff = vec[0:1, :], vec[1:2, :], vec[2:3, :], vec[3:4, :]
    row_of_slot = jnp.sum(
        jnp.where(iota((fslots, LANES), 0) == out_slot, frow + 1.0, 0.0), axis=1, keepdims=True
    ) - 1.0
    pick = ones_where(row_of_slot == iota((fslots, rows), 1))
    last = quarter - 1
    pair = NZ * FCAP
    line = nplane * FCAP
    in_plane = pl.ds(pl.multiple_of(plane * pair, pair), pair)
    in_line = pl.ds(pl.multiple_of(zpos * line, line), line)

    turn = lax.broadcasted_iota(jnp.int32, (fslots, fslots), 0)
    turned = ((turn // FCAP) & (nplane - 1)) * pair + turn // line * FCAP + (turn & (FCAP - 1))
    regroup[...] = ones_where(turned == lax.broadcasted_iota(jnp.int32, (fslots, fslots), 1))
    back = ((turn // FCAP) & (NZ - 1)) * line + turn // pair * FCAP + (turn & (FCAP - 1))
    ungroup[...] = ones_where(back == lax.broadcasted_iota(jnp.int32, (fslots, fslots), 1))

    def gather(q):
        for load in load_modes[q]:
            load.wait()
        got = dot(pick, whole[q][own_blocks].reshape(rows, 2 * LANES))
        for e in range(2):
            j = e * quarter + q
            over_plane[j] = got[:, e * LANES : (e + 1) * LANES].astype(bf16)
            if q < last:
                plane_recv[j, in_plane, :] = over_plane[j, in_plane, :]

    def send_over_plane(j):
        def send(k, carry):
            dest = lax.rem(plane + k, nplane)
            pltpu.make_async_remote_copy(
                over_plane.at[j, pl.ds(pl.multiple_of(dest * pair, pair), pair)],
                plane_recv.at[j, in_plane],
                plane_sem, plane_recv_sem.at[j], **to(dest * NZ + zpos, half),
            ).start()
            return carry

        lax.fori_loop(1, nplane, send, 0, unroll=15)

    gather(0)

    pl.semaphore_wait(barrier, NZ - 1 + 2 * nplane - 1)
    modes_copies = [
        pltpu.make_async_remote_copy(
            whole[q].at[own_blocks], whole[q].at[own_blocks], modes_sem.at[0, q], modes_sem.at[1, q],
            **to(comp, other),
        )
        for q in range(quarter)
    ]
    def send_all():
        for e in range(2):
            send_over_plane(e * quarter)
        gather(last)
        for e in range(2):
            j = e * quarter + last
            over_z[j] = dot(regroup[...], over_plane[j]).astype(bf16)
            send_over_z(j)
        modes_copies[0].start()
        for q in range(1, last):
            gather(q)
            for e in range(2):
                send_over_plane(e * quarter + q)
            modes_copies[q].start()
        modes_copies[last].start()

    def plane_wait(j):
        landed = plane_recv.at[j, pl.ds(0, (nplane - 1) * pair)]
        return pltpu.make_async_remote_copy(
            landed, landed, plane_sem, plane_recv_sem.at[j], **to(comp, other)
        )

    def z_wait(j):
        landed = z_recv.at[j, pl.ds(0, (NZ - 1) * line)]
        return pltpu.make_async_remote_copy(
            landed, landed, z_sem, z_recv_sem.at[j], **to(comp, other)
        )

    def pass_on(q):
        for e in range(2):
            pass_chunk(e * quarter + q)

    def send_over_z(j):
        z_recv[j, in_line, :] = over_z[j, in_line, :]

        def send(k, carry):
            dest = lax.rem(zpos + k, NZ)
            pltpu.make_async_remote_copy(
                over_z.at[j, pl.ds(pl.multiple_of(dest * line, line), line)],
                z_recv.at[j, in_line],
                z_sem, z_recv_sem.at[j], **to(plane * NZ + dest, half),
            ).start()
            return carry

        lax.fori_loop(1, NZ, send, 0, unroll=7)

    def pass_chunk(j):
        if j % quarter < last:
            plane_wait(j).wait_recv()
            over_z[j] = dot(regroup[...], plane_recv[j]).astype(bf16)
            send_over_z(j)
        else:
            z_wait(j).wait_recv()
            over_plane[j] = dot(ungroup[...], z_recv[j]).astype(bf16)
            plane_recv[j, in_plane, :] = over_plane[j, in_plane, :]
            send_over_plane(j)

    send_all()

    pass_on(0)

    for load in loads[4:7]:
        load.wait()
    owner = joint_owner[...].astype(f32)
    local = joint_local[...].astype(f32)
    njoint = owner.shape[1]
    square = (njoint, njoint)
    before = (as_column(owner) == owner) & (iota(square, 0) < iota(square, 1))
    position = jnp.sum(jnp.where(before, 1.0, 0.0), axis=0, keepdims=True)
    group = NZ * JCAP
    unit = group // 2
    owner_z = joint_owner[...] & (NZ - 1)
    owner_plane = joint_owner[...] // NZ
    slot_in_unit = (owner_z // 2) * JCAP + position.astype(jnp.int32)
    jslot = (owner_plane * group + (owner_z & 1) * unit + slot_in_unit).astype(f32)
    lane = slot_in_unit + (plane & 7) * unit
    of_plane = ones_where(
        lax.broadcasted_iota(jnp.int32, (2 * nplane, njoint), 0) == owner_plane * 2 + (owner_z & 1)
    )
    at_lane = jnp.where(
        lax.broadcasted_iota(jnp.int32, (LANES, njoint), 0) == lane, local + 1.0, 0.0
    ).astype(bf16)
    ids = lax.dot_general(of_plane, at_lane, (((1,), (1,)), ((), ())), preferred_element_type=f32)
    for d in range(2 * nplane):
        id_send[d] = ids[d : d + 1, :]
    id_recv[pl.ds(2 * here, 2)] = id_send[pl.ds(2 * plane, 2)]

    def id_copy(k, b):
        dest = lax.rem(plane + k, nplane)
        return pltpu.make_async_remote_copy(
            id_send.at[pl.ds(2 * dest, 2)], id_recv.at[pl.ds(2 * here, 2)],
            id_sem.at[0], id_sem.at[1], **to(dest * NZ + zpos, b),
        )

    def send_ids(k, carry):
        id_copy(k, half).start()
        id_copy(k, other).start()
        return carry

    id_copy(0, other).start()
    lax.fori_loop(1, nplane, send_ids, 0, unroll=15)

    at_row = iota((rows, LANES), 0) == frow
    slot_of_row = jnp.sum(jnp.where(at_row, in_slot + 1.0, 0.0), axis=1, keepdims=True) - 1.0
    bolt[...] = jnp.broadcast_to(
        jnp.sum(jnp.where(at_row, fstiff, 0.0), axis=1, keepdims=True), bolt.shape
    )
    select_row[...] = ones_where(slot_of_row == iota((rows, fslots), 1))
    by_row = as_column(frow) == iota((LANES, rows), 1)
    slots_along = jnp.sum(jnp.where(by_row, as_column(in_slot) + 1.0, 0.0), axis=0, keepdims=True)
    bolts_along = jnp.sum(jnp.where(by_row, as_column(fstiff), 0.0), axis=0, keepdims=True)
    takes = as_column(joint_rows[...].astype(f32)) == iota((njoint, rows), 1)
    joint_select[...] = ones_where(takes)
    joint_slot = jnp.sum(jnp.where(takes, slots_along, 0.0), axis=1, keepdims=True) - 1.0
    joint_flange[...] = ones_where(joint_slot == iota((njoint, fslots), 1))
    joint_bolt[...] = jnp.broadcast_to(
        jnp.sum(jnp.where(takes, bolts_along, 0.0), axis=1, keepdims=True), joint_bolt.shape
    )
    joint_place[...] = ones_where(iota((jslots, njoint), 0) == jslot)

    loads[7].wait()
    load_stiff.wait()


    def block_row(q):
        def run(r, carry):
            at = pl.ds(pl.multiple_of(r * BLOCK, BLOCK), BLOCK)
            taken = jnp.concatenate([whole[q][block_cols[0, k, r]] for k in range(NEIGH)], axis=0)
            own = whole[q][half * nblocks + r].astype(f32)
            value = dot(stiff[at, :], taken)
            for e in range(2):
                span = slice(e * LANES, (e + 1) * LANES)
                here_value = value[:, span] + bolt[at, :] * own[:, span]
                top = here_value.astype(bf16)
                base[e, q, at, :] = here_value
                high[e, q, at, :] = top
                low[e, q, at, :] = (here_value - top.astype(f32)).astype(bf16)
            return carry

        return run

    def product(q):
        modes_copies[q].wait()
        lax.fori_loop(0, nblocks, block_row(q), 0, unroll=16)
        sides = [jnp.concatenate([part[0, q], part[1, q]], axis=1) for part in (high, low)]
        joint_base[q] = dot(joint_select[...], sides[0]) + dot(joint_select[...], sides[1])

    def rows_copy(k, e, jj, g):
        dest = lax.rem(plane + k, nplane)
        return pltpu.make_async_remote_copy(
            rows_send.at[e * quarter + jj, pl.ds(pl.multiple_of(dest * group + g * unit, unit), unit)],
            rows_recv.at[jj, g, pl.ds(pl.multiple_of(here * unit, unit), unit)],
            rows_send_sem, rows_recv_sem.at[2 * jj + g], **to(dest * NZ + zpos, jnp.int32(e)),
        )

    def send_rows(e, jj, g):
        def send(k, carry):
            rows_copy(k, e, jj, g).start()
            return carry

        lax.fori_loop(1, nplane, send, 0, unroll=15)

        @pl.when(half != e)
        def _():
            rows_copy(0, e, jj, g).start()

        @pl.when(half == e)
        def _():
            rows_recv[jj, g, pl.ds(pl.multiple_of(here * unit, unit), unit), :] = rows_send[
                e * quarter + jj, pl.ds(pl.multiple_of(plane * group + g * unit, unit), unit), :
            ]

    def joint_rows_out(jj):
        span = slice(jj * LANES, (jj + 1) * LANES)
        for e in range(2):
            j = e * quarter + jj
            if jj < last:
                z_wait(j).wait_recv()
                part = z_recv[j]
            else:
                plane_wait(j).wait_recv()
                part = dot(regroup[...], plane_recv[j]).astype(bf16)
            incoming[e, :, span] = part
            entries = (
                joint_base[jj, :, e * LANES : (e + 1) * LANES]
                - joint_bolt[...] * dot(joint_flange[...], part)
            ).astype(bf16)
            rows_send[j] = dot(joint_place[...], entries).astype(bf16)
            send_rows(e, jj, 0)
        for e in range(2):
            send_rows(e, jj, 1)

    product(0)
    pass_on(1)
    joint_rows_out(0)
    pass_on(2)
    pass_on(3)
    product(1)
    joint_rows_out(1)
    product(2)

    id_all = id_recv.at[pl.ds(0, 2 * (2 * nplane - 1))]
    id_wait = pltpu.make_async_remote_copy(
        id_all, id_all, id_sem.at[0], id_sem.at[1], **to(comp, other)
    )
    id_wait.wait_recv()
    lane_z = ((lax.broadcasted_iota(jnp.int32, (1, LANES), 1) & (unit - 1)) // JCAP).astype(f32)
    sources = LANES // unit
    for g in range(2):
        for b in range(2 * nplane // sources):
            one = id_recv[2 * sources * b + g]
            for i in range(1, sources):
                one = one + id_recv[2 * (sources * b + i) + g]
            key = jnp.where(one > 0.5, lane_z * JOWN + one - 1.0, -1.0)
            place[g, :, b * LANES : (b + 1) * LANES] = ones_where(
                iota((NZ // 2 * JOWN, LANES), 0) == key
            )

    factor = 1.0 / math.sqrt(2 * rows)
    got_rows = pl.ds(0, (2 * nplane - 1) * unit)

    def add_up(jj, g):
        landed = rows_recv.at[jj, g, got_rows]
        pltpu.make_async_remote_copy(
            landed, landed, rows_send_sem, rows_recv_sem.at[2 * jj + g], **to(comp, other)
        ).wait_recv()
        part_send[jj, g] = dot(place[g], rows_recv[jj, g]).astype(bf16)
        mine = pl.ds(pl.multiple_of(zpos * JOWN, JOWN), JOWN)
        for q in range(NZ // 2):
            dest = 2 * q + g
            rows_there = pl.ds(q * JOWN, JOWN)

            @pl.when(dest != zpos)
            def _():
                pltpu.make_async_remote_copy(
                    part_send.at[jj, g, rows_there],
                    part_recv.at[jj, mine],
                    part_send_sem, part_recv_sem.at[jj], **to(plane * NZ + dest, half),
                ).start()

            @pl.when(dest == zpos)
            def _():
                part_recv[jj, mine, :] = part_send[jj, g, rows_there, :]

    def project(q):
        full = lax.dot_general(
            whole[q][...].reshape(2 * rows, 2 * LANES), round_full[...], (((0,), (0,)), ((), ())),
            preferred_element_type=f32,
        )
        for e in range(2):
            reduced[0, e * cols + q * LANES : e * cols + (q + 1) * LANES, :] = (
                full[e * LANES : (e + 1) * LANES] * factor
            )

    step = 256

    def round_rows(which, m, target, first):
        at = pl.ds(pl.multiple_of(m * step, step), step)
        partner = dot(select_row[at, :], incoming[which])
        for q in range(quarter):
            span = slice(q * LANES, (q + 1) * LANES)
            target[pl.ds(pl.multiple_of(first + m * step, step), step), span] = (
                base[which, q, at, :] - bolt[at, :] * partner[:, span]
            ).astype(bf16)

    def round_other(m, carry):
        round_rows(other, m, round_send, 0)
        return carry

    def round_own(m, carry):
        round_rows(half, m, round_full, half * rows)
        return carry

    round_copy = pltpu.make_async_remote_copy(
        round_send, round_full.at[own_rows], round_sem.at[0], round_sem.at[1], **to(comp, other)
    )

    add_up(0, 0)
    add_up(0, 1)
    joint_rows_out(2)
    product(3)
    joint_rows_out(3)
    add_up(1, 0)
    add_up(1, 1)
    lax.fori_loop(0, rows // step, round_other, 0)
    round_copy.start()
    add_up(2, 0)
    lax.fori_loop(0, rows // step, round_own, 0)
    add_up(2, 1)
    round_copy.wait()
    project(0)
    add_up(3, 0)
    project(1)
    add_up(3, 1)
    project(2)
    project(3)

    for jj in range(quarter):
        landed = part_recv.at[jj, pl.ds(0, (NZ - 1) * JOWN)]
        pltpu.make_async_remote_copy(
            landed, landed, part_send_sem, part_recv_sem.at[jj], **to(comp, other)
        ).wait_recv()
        total = part_recv[jj, 0:JOWN, :].astype(f32)
        for z in range(1, NZ):
            total = total + part_recv[jj, z * JOWN : (z + 1) * JOWN, :].astype(f32)
        forces[:, jj * LANES : (jj + 1) * LANES] = total

    for j in range(chunks):
        plane_wait(j).wait_send()
        z_wait(j).wait_send()
    id_wait.wait_send()

    for jj in range(quarter):
        for g in range(2):
            gone = rows_recv.at[jj, g, got_rows]
            pltpu.make_async_remote_copy(
                gone, gone, rows_send_sem, rows_recv_sem.at[2 * jj + g], **to(comp, other)
            ).wait_send()
        gone = part_recv.at[jj, pl.ds(0, (NZ - 1) * JOWN)]
        pltpu.make_async_remote_copy(
            gone, gone, part_send_sem, part_recv_sem.at[jj], **to(comp, other)
        ).wait_send()


def store(reduced, forces, reduced_hbm, forces_hbm, sem):
    copies = [
        pltpu.make_async_copy(reduced, reduced_hbm, sem.at[0]),
        pltpu.make_async_copy(forces, forces_hbm, sem.at[1]),
    ]
    for copy in copies:
        copy.start()
    for copy in copies:
        copy.wait()


def body(*args):
    modes, stiff = args[0], args[1]
    ncomp = lax.axis_size("comp")
    rows, iface = modes.shape[1:]
    cols = iface // 2
    quarter = cols // LANES
    chunks = 2 * quarter
    width, njoint = stiff.shape[2], args[7].shape[1]
    fslots, jslots = ncomp * FCAP, ncomp * JCAP
    nplane = ncomp // NZ
    dma = pltpu.SemaphoreType.DMA
    vmem = pl.BlockSpec(memory_space=pltpu.VMEM)
    hbm = pl.BlockSpec(memory_space=pl.ANY)
    scratch = [pltpu.SMEM((1, NEIGH, rows // BLOCK), jnp.int32)]
    scratch += [pltpu.VMEM(a.shape, a.dtype) for a in args[3:]]
    scratch += [pltpu.VMEM((2 * rows // BLOCK, BLOCK, 2 * LANES), bf16)] * quarter
    scratch += [
        pltpu.VMEM((rows, width), bf16),
        pltpu.VMEM((8, LANES), f32),
        pltpu.VMEM((chunks, fslots, LANES), bf16),
        pltpu.VMEM((chunks, fslots, LANES), bf16),
        pltpu.VMEM((fslots, fslots), bf16),
        pltpu.VMEM((fslots, fslots), bf16),
        pltpu.VMEM((chunks, fslots, LANES), bf16),
        pltpu.VMEM((chunks, fslots, LANES), bf16),
        pltpu.VMEM((2, fslots, cols), bf16),
        pltpu.VMEM((2, quarter, rows, LANES), f32),
        pltpu.VMEM((2, quarter, rows, LANES), bf16),
        pltpu.VMEM((2, quarter, rows, LANES), bf16),
        pltpu.VMEM((rows, LANES), f32),
        pltpu.VMEM((rows, fslots), bf16),
        pltpu.VMEM((njoint, rows), bf16),
        pltpu.VMEM((njoint, fslots), bf16),
        pltpu.VMEM((njoint, LANES), f32),
        pltpu.VMEM((jslots, njoint), bf16),
        pltpu.VMEM((quarter, njoint, 2 * LANES), f32),
        pltpu.VMEM((2 * nplane, 1, LANES), f32),
        pltpu.VMEM((4 * nplane, 1, LANES), f32),
        pltpu.VMEM((2, NZ // 2 * JOWN, jslots), bf16),
        pltpu.VMEM((2 * quarter, jslots, LANES), bf16),
        pltpu.VMEM((quarter, 2, jslots, LANES), bf16),
        pltpu.VMEM((rows, cols), bf16),
        pltpu.VMEM((2 * rows, cols), bf16),
        pltpu.VMEM((quarter, 2, NZ // 2 * JOWN, LANES), bf16),
        pltpu.VMEM((quarter, NZ * JOWN, LANES), bf16),
        dma((chunks + 1,)), dma((8,)), dma, dma((chunks,)), dma, dma((chunks,)),
        dma((2, quarter)), dma((2,)), dma, dma((chunks,)),
        dma((2,)), dma, dma((quarter,)),
    ]
    results = pl.pallas_call(
        kernel,
        out_shape=(
            pltpu.VMEM((1, iface, cols), f32),
            pltpu.VMEM((JOWN, cols), f32),
        ),
        in_specs=[hbm] * 10,
        out_specs=(vmem, vmem),
        scratch_shapes=scratch,
        compiler_params=pltpu.CompilerParams(
            collective_id=0, has_side_effects=True, vmem_limit_bytes=56 << 20
        ),
    )(modes.reshape(rows // BLOCK, BLOCK, iface), stiff, jnp.swapaxes(args[2], 1, 2), *args[3:])
    return pl.pallas_call(
        store,
        out_shape=tuple(jax.ShapeDtypeStruct(r.shape, r.dtype) for r in results),
        in_specs=[vmem, vmem],
        out_specs=(hbm, hbm),
        scratch_shapes=[dma((2,))],
    )(*(pltpu.with_memory_space_constraint(r, pltpu.VMEM) for r in results))


def solution(mesh):
    placed = (
        P("comp", "blk", None),
        P("comp", "blk", None),
        P("comp", "blk", None),
        P("comp", "blk"),
        P("comp", "blk"),
        P("comp", "blk"),
        P("comp", "blk"),
        P("comp", "blk"),
        P("comp", "blk"),
        P("comp", "blk"),
    )
    return jax.shard_map(
        body,
        mesh=mesh,
        in_specs=placed,
        out_specs=(P("comp", None, "blk"), P("comp", "blk")),
        check_vma=False,
    )
```

```python
import math

import jax
import jax.numpy as jnp
from jax import lax
from jax.experimental import pallas as pl
from jax.experimental.pallas import tpu as pltpu
from jax.sharding import PartitionSpec as P

MESH = pl.DeviceIdType.MESH
BLOCK = 64
NEIGH = 8
FCAP = 2
JCAP = 4
JOWN = 64
NZ = 8
LANES = 128
f32 = jnp.float32
bf16 = jnp.bfloat16


def iota(shape, dim):
    return lax.broadcasted_iota(jnp.int32, shape, dim).astype(f32)


def ones_where(mask):
    return jnp.where(mask, 1.0, 0.0).astype(bf16)


def dot(left, right):
    return jnp.dot(left, right, preferred_element_type=f32)


def as_column(row):
    n = row.shape[1]
    return jnp.sum(jnp.where(iota((n, n), 0) == iota((n, n), 1), row, 0.0), axis=1, keepdims=True)


def kernel(
    modes_hbm, stiff_hbm, block_cols_hbm, flange_rows_hbm, flange_dest_hbm, flange_match_hbm,
    flange_stiff_hbm, joint_rows_hbm, joint_owner_hbm, joint_local_hbm,
    reduced, forces,
    block_cols, flange_rows, flange_dest, flange_match, flange_stiff,
    joint_rows, joint_owner, joint_local,
    whole_0, whole_1, whole_2, whole_3, stiff, vec, over_plane, plane_recv, regroup, ungroup, over_z, z_recv, incoming, base, high, low,
    bolt, select_row, joint_select, joint_flange, joint_bolt, joint_place, joint_base,
    id_send, id_recv, place, rows_send, rows_recv, round_send, round_full,
    part_send, part_recv,
    load_sem, small_sem, plane_sem, plane_recv_sem, z_sem, z_recv_sem, modes_sem, id_sem, rows_send_sem, rows_recv_sem,
    round_sem, part_send_sem, part_recv_sem,
):
    ncomp = lax.axis_size("comp")
    nplane = ncomp // NZ
    comp = lax.axis_index("comp")
    half = lax.axis_index("blk")
    other = 1 - half
    plane = comp // NZ
    zpos = lax.rem(comp, NZ)
    whole = (whole_0, whole_1, whole_2, whole_3)
    rows, cols = stiff.shape[0], forces.shape[1]
    iface = 2 * cols
    nflange = flange_rows.shape[1]
    fslots = ncomp * FCAP
    jslots = ncomp * JCAP
    chunks = iface // LANES
    quarter = chunks // 2
    own_rows = pl.ds(pl.multiple_of(half * rows, rows), rows)
    nblocks = rows // BLOCK
    own_blocks = pl.ds(half * nblocks, nblocks)
    here = half * nplane + plane

    def to(c, b):
        return dict(device_id={"comp": c, "blk": b}, device_id_type=MESH)

    load_modes = [
        [
            pltpu.make_async_copy(
                modes_hbm.at[:, :, pl.ds(e * cols + q * LANES, LANES)],
                whole[q].at[own_blocks, :, pl.ds(e * LANES, LANES)],
                load_sem.at[2 * q + e],
            )
            for e in range(2)
        ]
        for q in range(quarter)
    ]
    load_stiff = pltpu.make_async_copy(stiff_hbm.at[0], stiff, load_sem.at[chunks])
    loads = [
        pltpu.make_async_copy(source, target, small_sem.at[i])
        for i, (source, target) in enumerate(
            (
                (flange_rows_hbm, flange_rows),
                (flange_dest_hbm, flange_dest),
                (flange_match_hbm, flange_match),
                (flange_stiff_hbm, flange_stiff),
                (joint_rows_hbm, joint_rows),
                (joint_owner_hbm, joint_owner),
                (joint_local_hbm, joint_local),
                (block_cols_hbm, block_cols),
            )
        )
    ]
    for load in loads[:4]:
        load.start()
    for q in range(quarter):
        for load in load_modes[q]:
            load.start()
    for load in loads[4:]:
        load.start()
    load_stiff.start()

    barrier = pltpu.get_barrier_semaphore()

    def greet_z(k, carry):
        pl.semaphore_signal(barrier, inc=1, **to(plane * NZ + lax.rem(zpos + k, NZ), half))
        return carry

    def greet_plane(k, carry):
        there = lax.rem(plane + k, nplane) * NZ + zpos
        pl.semaphore_signal(barrier, inc=1, **to(there, other))
        pl.semaphore_signal(barrier, inc=1, **to(there, half))
        return carry

    lax.fori_loop(1, NZ, greet_z, 0, unroll=7)
    lax.fori_loop(1, nplane, greet_plane, 0, unroll=15)
    pl.semaphore_signal(barrier, inc=1, **to(comp, other))

    for load in loads[:4]:
        load.wait()
    vec[...] = jnp.full(vec.shape, -1.0, f32)
    parity = lax.broadcasted_iota(jnp.int32, (1, nflange), 1) & 1
    vec[0:1, 0:nflange] = flange_rows[...].astype(f32)
    vec[1:2, 0:nflange] = (flange_dest[...] * FCAP + parity).astype(f32)
    vec[2:3, 0:nflange] = (
        ((flange_dest[...] & (NZ - 1)) * nplane + flange_dest[...] // NZ) * FCAP
        + (flange_match[...] & 1)
    ).astype(f32)
    vec[3:4, 0:nflange] = flange_stiff[...]
    frow, out_slot, in_slot, fstiff = vec[0:1, :], vec[1:2, :], vec[2:3, :], vec[3:4, :]
    pick = ones_where(as_column(frow) == iota((LANES, rows), 1))
    into_slot = ones_where(iota((fslots, LANES), 0) == out_slot)
    last = quarter - 1
    pair = NZ * FCAP
    line = nplane * FCAP
    in_plane = pl.ds(pl.multiple_of(plane * pair, pair), pair)
    in_line = pl.ds(pl.multiple_of(zpos * line, line), line)

    turn = lax.broadcasted_iota(jnp.int32, (fslots, fslots), 0)
    turned = ((turn // FCAP) & (nplane - 1)) * pair + turn // line * FCAP + (turn & (FCAP - 1))
    regroup[...] = ones_where(turned == lax.broadcasted_iota(jnp.int32, (fslots, fslots), 1))
    back = ((turn // FCAP) & (NZ - 1)) * line + turn // pair * FCAP + (turn & (FCAP - 1))
    ungroup[...] = ones_where(back == lax.broadcasted_iota(jnp.int32, (fslots, fslots), 1))

    def gather(q):
        for load in load_modes[q]:
            load.wait()
        nodes = dot(pick, whole[q][own_blocks].reshape(rows, 2 * LANES)).astype(bf16)
        got = dot(into_slot, nodes)
        for e in range(2):
            j = e * quarter + q
            over_plane[j] = got[:, e * LANES : (e + 1) * LANES].astype(bf16)
            if q < last:
                plane_recv[j, in_plane, :] = over_plane[j, in_plane, :]

    def send_over_plane(j):
        def send(k, carry):
            dest = lax.rem(plane + k, nplane)
            pltpu.make_async_remote_copy(
                over_plane.at[j, pl.ds(pl.multiple_of(dest * pair, pair), pair)],
                plane_recv.at[j, in_plane],
                plane_sem, plane_recv_sem.at[j], **to(dest * NZ + zpos, half),
            ).start()
            return carry

        lax.fori_loop(1, nplane, send, 0, unroll=15)

    gather(0)

    pl.semaphore_wait(barrier, NZ - 1 + 2 * nplane - 1)
    modes_copies = [
        pltpu.make_async_remote_copy(
            whole[q].at[own_blocks], whole[q].at[own_blocks], modes_sem.at[0, q], modes_sem.at[1, q],
            **to(comp, other),
        )
        for q in range(quarter)
    ]
    def send_all():
        for e in range(2):
            send_over_plane(e * quarter)
        gather(last)
        for e in range(2):
            j = e * quarter + last
            over_z[j] = dot(regroup[...], over_plane[j]).astype(bf16)
            send_over_z(j)
        modes_copies[0].start()
        for q in range(1, last):
            gather(q)
            for e in range(2):
                send_over_plane(e * quarter + q)
            modes_copies[q].start()
        modes_copies[last].start()

    def plane_wait(j):
        landed = plane_recv.at[j, pl.ds(0, (nplane - 1) * pair)]
        return pltpu.make_async_remote_copy(
            landed, landed, plane_sem, plane_recv_sem.at[j], **to(comp, other)
        )

    def z_wait(j):
        landed = z_recv.at[j, pl.ds(0, (NZ - 1) * line)]
        return pltpu.make_async_remote_copy(
            landed, landed, z_sem, z_recv_sem.at[j], **to(comp, other)
        )

    def pass_on(q):
        for e in range(2):
            pass_chunk(e * quarter + q)

    def send_over_z(j):
        z_recv[j, in_line, :] = over_z[j, in_line, :]

        def send(k, carry):
            dest = lax.rem(zpos + k, NZ)
            pltpu.make_async_remote_copy(
                over_z.at[j, pl.ds(pl.multiple_of(dest * line, line), line)],
                z_recv.at[j, in_line],
                z_sem, z_recv_sem.at[j], **to(plane * NZ + dest, half),
            ).start()
            return carry

        lax.fori_loop(1, NZ, send, 0, unroll=7)

    def pass_chunk(j):
        if j % quarter < last:
            plane_wait(j).wait_recv()
            over_z[j] = dot(regroup[...], plane_recv[j]).astype(bf16)
            send_over_z(j)
        else:
            z_wait(j).wait_recv()
            over_plane[j] = dot(ungroup[...], z_recv[j]).astype(bf16)
            plane_recv[j, in_plane, :] = over_plane[j, in_plane, :]
            send_over_plane(j)

    send_all()

    pass_on(0)

    for load in loads[4:7]:
        load.wait()
    owner = joint_owner[...].astype(f32)
    local = joint_local[...].astype(f32)
    njoint = owner.shape[1]
    square = (njoint, njoint)
    before = (as_column(owner) == owner) & (iota(square, 0) < iota(square, 1))
    position = jnp.sum(jnp.where(before, 1.0, 0.0), axis=0, keepdims=True)
    group = NZ * JCAP
    unit = group // 2
    owner_z = joint_owner[...] & (NZ - 1)
    owner_plane = joint_owner[...] // NZ
    slot_in_unit = (owner_z // 2) * JCAP + position.astype(jnp.int32)
    jslot = (owner_plane * group + (owner_z & 1) * unit + slot_in_unit).astype(f32)
    lane = slot_in_unit + (plane & 7) * unit
    of_plane = ones_where(
        lax.broadcasted_iota(jnp.int32, (2 * nplane, njoint), 0) == owner_plane * 2 + (owner_z & 1)
    )
    at_lane = jnp.where(
        lax.broadcasted_iota(jnp.int32, (LANES, njoint), 0) == lane, local + 1.0, 0.0
    ).astype(bf16)
    ids = lax.dot_general(of_plane, at_lane, (((1,), (1,)), ((), ())), preferred_element_type=f32)
    for d in range(2 * nplane):
        id_send[d] = ids[d : d + 1, :]
    id_recv[pl.ds(2 * here, 2)] = id_send[pl.ds(2 * plane, 2)]

    def id_copy(k, b):
        dest = lax.rem(plane + k, nplane)
        return pltpu.make_async_remote_copy(
            id_send.at[pl.ds(2 * dest, 2)], id_recv.at[pl.ds(2 * here, 2)],
            id_sem.at[0], id_sem.at[1], **to(dest * NZ + zpos, b),
        )

    def send_ids(k, carry):
        id_copy(k, half).start()
        id_copy(k, other).start()
        return carry

    id_copy(0, other).start()
    lax.fori_loop(1, nplane, send_ids, 0, unroll=15)

    at_row = iota((rows, LANES), 0) == frow
    slot_of_row = jnp.sum(jnp.where(at_row, in_slot + 1.0, 0.0), axis=1, keepdims=True) - 1.0
    bolt[...] = jnp.broadcast_to(
        jnp.sum(jnp.where(at_row, fstiff, 0.0), axis=1, keepdims=True), bolt.shape
    )
    select_row[...] = ones_where(slot_of_row == iota((rows, fslots), 1))
    by_row = as_column(frow) == iota((LANES, rows), 1)
    slots_along = jnp.sum(jnp.where(by_row, as_column(in_slot) + 1.0, 0.0), axis=0, keepdims=True)
    bolts_along = jnp.sum(jnp.where(by_row, as_column(fstiff), 0.0), axis=0, keepdims=True)
    takes = as_column(joint_rows[...].astype(f32)) == iota((njoint, rows), 1)
    joint_select[...] = ones_where(takes)
    joint_slot = jnp.sum(jnp.where(takes, slots_along, 0.0), axis=1, keepdims=True) - 1.0
    joint_flange[...] = ones_where(joint_slot == iota((njoint, fslots), 1))
    joint_bolt[...] = jnp.broadcast_to(
        jnp.sum(jnp.where(takes, bolts_along, 0.0), axis=1, keepdims=True), joint_bolt.shape
    )
    joint_place[...] = ones_where(iota((jslots, njoint), 0) == jslot)

    loads[7].wait()
    load_stiff.wait()


    def block_row(q):
        def run(r, carry):
            at = pl.ds(pl.multiple_of(r * BLOCK, BLOCK), BLOCK)
            taken = jnp.concatenate([whole[q][block_cols[0, k, r]] for k in range(NEIGH)], axis=0)
            own = whole[q][half * nblocks + r].astype(f32)
            value = dot(stiff[at, :], taken)
            for e in range(2):
                span = slice(e * LANES, (e + 1) * LANES)
                here_value = value[:, span] + bolt[at, :] * own[:, span]
                top = here_value.astype(bf16)
                base[e, q, at, :] = here_value
                high[e, q, at, :] = top
                low[e, q, at, :] = (here_value - top.astype(f32)).astype(bf16)
            return carry

        return run

    def product(q):
        modes_copies[q].wait()
        lax.fori_loop(0, nblocks, block_row(q), 0, unroll=16)
        sides = [jnp.concatenate([part[0, q], part[1, q]], axis=1) for part in (high, low)]
        joint_base[q] = dot(joint_select[...], sides[0]) + dot(joint_select[...], sides[1])

    def rows_copy(k, e, jj, g):
        dest = lax.rem(plane + k, nplane)
        return pltpu.make_async_remote_copy(
            rows_send.at[e * quarter + jj, pl.ds(pl.multiple_of(dest * group + g * unit, unit), unit)],
            rows_recv.at[jj, g, pl.ds(pl.multiple_of(here * unit, unit), unit)],
            rows_send_sem, rows_recv_sem.at[2 * jj + g], **to(dest * NZ + zpos, jnp.int32(e)),
        )

    def send_rows(e, jj, g):
        def send(k, carry):
            rows_copy(k, e, jj, g).start()
            return carry

        lax.fori_loop(1, nplane, send, 0, unroll=15)

        @pl.when(half != e)
        def _():
            rows_copy(0, e, jj, g).start()

        @pl.when(half == e)
        def _():
            rows_recv[jj, g, pl.ds(pl.multiple_of(here * unit, unit), unit), :] = rows_send[
                e * quarter + jj, pl.ds(pl.multiple_of(plane * group + g * unit, unit), unit), :
            ]

    def joint_rows_out(jj):
        span = slice(jj * LANES, (jj + 1) * LANES)
        for e in range(2):
            j = e * quarter + jj
            if jj < last:
                z_wait(j).wait_recv()
                part = z_recv[j]
            else:
                plane_wait(j).wait_recv()
                part = dot(regroup[...], plane_recv[j]).astype(bf16)
            incoming[e, :, span] = part
            entries = (
                joint_base[jj, :, e * LANES : (e + 1) * LANES]
                - joint_bolt[...] * dot(joint_flange[...], part)
            ).astype(bf16)
            rows_send[j] = dot(joint_place[...], entries).astype(bf16)
            send_rows(e, jj, 0)
        for e in range(2):
            send_rows(e, jj, 1)

    product(0)
    pass_on(1)
    joint_rows_out(0)
    pass_on(2)
    pass_on(3)
    product(1)
    joint_rows_out(1)
    product(2)

    id_all = id_recv.at[pl.ds(0, 2 * (2 * nplane - 1))]
    id_wait = pltpu.make_async_remote_copy(
        id_all, id_all, id_sem.at[0], id_sem.at[1], **to(comp, other)
    )
    id_wait.wait_recv()
    lane_z = ((lax.broadcasted_iota(jnp.int32, (1, LANES), 1) & (unit - 1)) // JCAP).astype(f32)
    sources = LANES // unit
    for g in range(2):
        for b in range(2 * nplane // sources):
            one = id_recv[2 * sources * b + g]
            for i in range(1, sources):
                one = one + id_recv[2 * (sources * b + i) + g]
            key = jnp.where(one > 0.5, lane_z * JOWN + one - 1.0, -1.0)
            place[g, :, b * LANES : (b + 1) * LANES] = ones_where(
                iota((NZ // 2 * JOWN, LANES), 0) == key
            )

    factor = 1.0 / math.sqrt(2 * rows)
    got_rows = pl.ds(0, (2 * nplane - 1) * unit)

    def add_up(jj, g):
        landed = rows_recv.at[jj, g, got_rows]
        pltpu.make_async_remote_copy(
            landed, landed, rows_send_sem, rows_recv_sem.at[2 * jj + g], **to(comp, other)
        ).wait_recv()
        part_send[jj, g] = dot(place[g], rows_recv[jj, g]).astype(bf16)
        mine = pl.ds(pl.multiple_of(zpos * JOWN, JOWN), JOWN)
        for q in range(NZ // 2):
            dest = 2 * q + g
            rows_there = pl.ds(q * JOWN, JOWN)

            @pl.when(dest != zpos)
            def _():
                pltpu.make_async_remote_copy(
                    part_send.at[jj, g, rows_there],
                    part_recv.at[jj, mine],
                    part_send_sem, part_recv_sem.at[jj], **to(plane * NZ + dest, half),
                ).start()

            @pl.when(dest == zpos)
            def _():
                part_recv[jj, mine, :] = part_send[jj, g, rows_there, :]

    def project(q):
        full = lax.dot_general(
            whole[q][...].reshape(2 * rows, 2 * LANES), round_full[...], (((0,), (0,)), ((), ())),
            preferred_element_type=f32,
        )
        for e in range(2):
            reduced[0, e * cols + q * LANES : e * cols + (q + 1) * LANES, :] = (
                full[e * LANES : (e + 1) * LANES] * factor
            )

    step = 256

    def round_rows(which, m, target, first):
        at = pl.ds(pl.multiple_of(m * step, step), step)
        partner = dot(select_row[at, :], incoming[which])
        for q in range(quarter):
            span = slice(q * LANES, (q + 1) * LANES)
            target[pl.ds(pl.multiple_of(first + m * step, step), step), span] = (
                base[which, q, at, :] - bolt[at, :] * partner[:, span]
            ).astype(bf16)

    def round_other(m, carry):
        round_rows(other, m, round_send, 0)
        return carry

    def round_own(m, carry):
        round_rows(half, m, round_full, half * rows)
        return carry

    round_copy = pltpu.make_async_remote_copy(
        round_send, round_full.at[own_rows], round_sem.at[0], round_sem.at[1], **to(comp, other)
    )

    add_up(0, 0)
    add_up(0, 1)
    joint_rows_out(2)
    product(3)
    joint_rows_out(3)
    add_up(1, 0)
    add_up(1, 1)
    lax.fori_loop(0, rows // step, round_other, 0)
    round_copy.start()
    add_up(2, 0)
    lax.fori_loop(0, rows // step, round_own, 0)
    add_up(2, 1)
    round_copy.wait()
    project(0)
    add_up(3, 0)
    project(1)
    add_up(3, 1)
    project(2)
    project(3)

    for jj in range(quarter):
        landed = part_recv.at[jj, pl.ds(0, (NZ - 1) * JOWN)]
        pltpu.make_async_remote_copy(
            landed, landed, part_send_sem, part_recv_sem.at[jj], **to(comp, other)
        ).wait_recv()
        total = part_recv[jj, 0:JOWN, :].astype(f32)
        for z in range(1, NZ):
            total = total + part_recv[jj, z * JOWN : (z + 1) * JOWN, :].astype(f32)
        forces[:, jj * LANES : (jj + 1) * LANES] = total

    for j in range(chunks):
        plane_wait(j).wait_send()
        z_wait(j).wait_send()
    id_wait.wait_send()

    for jj in range(quarter):
        for g in range(2):
            gone = rows_recv.at[jj, g, got_rows]
            pltpu.make_async_remote_copy(
                gone, gone, rows_send_sem, rows_recv_sem.at[2 * jj + g], **to(comp, other)
            ).wait_send()
        gone = part_recv.at[jj, pl.ds(0, (NZ - 1) * JOWN)]
        pltpu.make_async_remote_copy(
            gone, gone, part_send_sem, part_recv_sem.at[jj], **to(comp, other)
        ).wait_send()


def store(reduced, forces, reduced_hbm, forces_hbm, sem):
    copies = [
        pltpu.make_async_copy(reduced, reduced_hbm, sem.at[0]),
        pltpu.make_async_copy(forces, forces_hbm, sem.at[1]),
    ]
    for copy in copies:
        copy.start()
    for copy in copies:
        copy.wait()


def body(*args):
    modes, stiff = args[0], args[1]
    ncomp = lax.axis_size("comp")
    rows, iface = modes.shape[1:]
    cols = iface // 2
    quarter = cols // LANES
    chunks = 2 * quarter
    width, njoint = stiff.shape[2], args[7].shape[1]
    fslots, jslots = ncomp * FCAP, ncomp * JCAP
    nplane = ncomp // NZ
    dma = pltpu.SemaphoreType.DMA
    vmem = pl.BlockSpec(memory_space=pltpu.VMEM)
    hbm = pl.BlockSpec(memory_space=pl.ANY)
    scratch = [pltpu.SMEM((1, NEIGH, rows // BLOCK), jnp.int32)]
    scratch += [pltpu.VMEM(a.shape, a.dtype) for a in args[3:]]
    scratch += [pltpu.VMEM((2 * rows // BLOCK, BLOCK, 2 * LANES), bf16)] * quarter
    scratch += [
        pltpu.VMEM((rows, width), bf16),
        pltpu.VMEM((8, LANES), f32),
        pltpu.VMEM((chunks, fslots, LANES), bf16),
        pltpu.VMEM((chunks, fslots, LANES), bf16),
        pltpu.VMEM((fslots, fslots), bf16),
        pltpu.VMEM((fslots, fslots), bf16),
        pltpu.VMEM((chunks, fslots, LANES), bf16),
        pltpu.VMEM((chunks, fslots, LANES), bf16),
        pltpu.VMEM((2, fslots, cols), bf16),
        pltpu.VMEM((2, quarter, rows, LANES), f32),
        pltpu.VMEM((2, quarter, rows, LANES), bf16),
        pltpu.VMEM((2, quarter, rows, LANES), bf16),
        pltpu.VMEM((rows, LANES), f32),
        pltpu.VMEM((rows, fslots), bf16),
        pltpu.VMEM((njoint, rows), bf16),
        pltpu.VMEM((njoint, fslots), bf16),
        pltpu.VMEM((njoint, LANES), f32),
        pltpu.VMEM((jslots, njoint), bf16),
        pltpu.VMEM((quarter, njoint, 2 * LANES), f32),
        pltpu.VMEM((2 * nplane, 1, LANES), f32),
        pltpu.VMEM((4 * nplane, 1, LANES), f32),
        pltpu.VMEM((2, NZ // 2 * JOWN, jslots), bf16),
        pltpu.VMEM((2 * quarter, jslots, LANES), bf16),
        pltpu.VMEM((quarter, 2, jslots, LANES), bf16),
        pltpu.VMEM((rows, cols), bf16),
        pltpu.VMEM((2 * rows, cols), bf16),
        pltpu.VMEM((quarter, 2, NZ // 2 * JOWN, LANES), bf16),
        pltpu.VMEM((quarter, NZ * JOWN, LANES), bf16),
        dma((chunks + 1,)), dma((8,)), dma, dma((chunks,)), dma, dma((chunks,)),
        dma((2, quarter)), dma((2,)), dma, dma((chunks,)),
        dma((2,)), dma, dma((quarter,)),
    ]
    results = pl.pallas_call(
        kernel,
        out_shape=(
            pltpu.VMEM((1, iface, cols), f32),
            pltpu.VMEM((JOWN, cols), f32),
        ),
        in_specs=[hbm] * 10,
        out_specs=(vmem, vmem),
        scratch_shapes=scratch,
        compiler_params=pltpu.CompilerParams(
            collective_id=0, has_side_effects=True, vmem_limit_bytes=56 << 20
        ),
    )(modes.reshape(rows // BLOCK, BLOCK, iface), stiff, jnp.swapaxes(args[2], 1, 2), *args[3:])
    return pl.pallas_call(
        store,
        out_shape=tuple(jax.ShapeDtypeStruct(r.shape, r.dtype) for r in results),
        in_specs=[vmem, vmem],
        out_specs=(hbm, hbm),
        scratch_shapes=[dma((2,))],
    )(*(pltpu.with_memory_space_constraint(r, pltpu.VMEM) for r in results))


def solution(mesh):
    placed = (
        P("comp", "blk", None),
        P("comp", "blk", None),
        P("comp", "blk", None),
        P("comp", "blk"),
        P("comp", "blk"),
        P("comp", "blk"),
        P("comp", "blk"),
        P("comp", "blk"),
        P("comp", "blk"),
        P("comp", "blk"),
    )
    return jax.shard_map(
        body,
        mesh=mesh,
        in_specs=placed,
        out_specs=(P("comp", None, "blk"), P("comp", "blk")),
        check_vma=False,
    )
```
